256 devices in a mesh: fsdp: 64 (over x, z, core), group: 4 (over y).
Axes of the slice: x: 4, y: 4, z: 8, core: 2. Of those that a mesh axis runs over, the one named last changes fastest.
Arguments:
- gradient: bfloat16 [16, 512, 8192], P(None, 'fsdp', 'group')
- second_moment: bfloat16 [16, 512, 8192], P(None, 'fsdp', 'group'), may hold values from 0.049804688 to 5
- left_root: bfloat16 [64, 4, 2, 512, 512], P('fsdp', 'group')
- right_root: bfloat16 [64, 4, 2, 512, 512], P('fsdp', 'group')
- block_owner: int32 [256], replicated, may hold values from 0 to 63, as said below
- row_offset: int32 [256], replicated, may hold values from 0 to 7680, as said below
- col_offset: int32 [256], replicated, may hold values from 0 to 7680, as said below
Outputs:
- update: bfloat16 [16, 512, 8192], P(None, 'fsdp')
- new_moment: bfloat16 [16, 512, 8192], P(None, 'fsdp', 'group')
- left_stat: float32 [64, 4, 2, 512, 512], P('fsdp', 'group')
- right_stat: float32 [64, 4, 2, 512, 512], P('fsdp', 'group')
The draws below stay inside these ranges and needn't reach their ends.
Inputs may be any that keep to these rules, and one draw needn't show every extreme that they name: row_offset and col_offset are multiples of 512; together they name each block position of the window exactly once. `col_offset`: see row_offset. `block_owner`: in each of the 4 column ranges, one owner holds at most 2 of that range's blocks; with m blocks in a range, m // 4 owners hold exactly 2 and m - 2 * (m // 4) further owners hold one each.
All inputs are finite; a program needn't handle non-finite values.
Results may differ from the reference program's by a relative error of at most 0.0049.
Values may be sent and summed in bfloat16 or wider, within the bound.
A program may use at most 64 MiB of HBM per device.

```python
import math
import jax
import jax.numpy as jnp
import numpy as np
from jax import lax

COLS = 8192
BLOCK = 512
SLOTS = 2
BANDS = 16
N_FSDP = 64
N_GROUP = 4


def block_layout(key):
    block_total = BANDS * (COLS // BLOCK)
    range_blocks = BANDS * (COLS // (N_GROUP * BLOCK))
    positions = jax.random.permutation(jax.random.fold_in(key, 101), block_total).astype(jnp.int32)
    col_index = positions % (COLS // BLOCK)
    band_index = positions // (COLS // BLOCK)
    col_range = col_index // (COLS // (N_GROUP * BLOCK))
    position = jnp.arange(block_total, dtype=jnp.int32)
    earlier = (col_range[:, None] == col_range[None, :]) & (position[None, :] < position[:, None])
    rank_within = jnp.sum(earlier.astype(jnp.int32), axis=1)
    paired = range_blocks // 4
    single = range_blocks - 2 * paired
    pattern = np.concatenate([np.repeat(np.arange(paired), 2), np.arange(paired, paired + single)]).astype(np.int32)
    owner_keys = jax.random.split(jax.random.fold_in(key, 102), N_GROUP)
    shuffle_keys = jax.random.split(jax.random.fold_in(key, 103), N_GROUP)
    owner_order = jax.vmap(lambda subkey: jax.random.permutation(subkey, N_FSDP))(owner_keys).astype(jnp.int32)
    shuffle = jax.vmap(lambda subkey: jax.random.permutation(subkey, range_blocks))(shuffle_keys)
    owner_lists = jnp.take_along_axis(owner_order, jnp.asarray(pattern)[shuffle], axis=1)
    owners = owner_lists[col_range, rank_within]
    return ((band_index * BLOCK).astype(jnp.int32), (col_index * BLOCK).astype(jnp.int32), owners.astype(jnp.int32))


def root_matrix(key, width):
    diag_key, off_key = jax.random.split(key)
    shape = (N_FSDP, N_GROUP, SLOTS, BLOCK, BLOCK)
    noise = jax.random.normal(off_key, shape, jnp.float32)
    symmetric = (noise + jnp.swapaxes(noise, -1, -2)) * (width * 0.7071 / np.sqrt(BLOCK))
    diagonal = jax.random.uniform(diag_key, (N_FSDP, N_GROUP, SLOTS, BLOCK), jnp.float32, 0.8, 1.2)
    eye = jnp.eye(BLOCK, dtype=jnp.float32)
    matrix = symmetric * (1.0 - eye) + diagonal[..., None] * eye
    return matrix.astype(jnp.bfloat16)


def draw_gradient(key, part):
    key = jax.random.fold_in(key, 7)
    base_key, row_key, col_key = jax.random.split(key, 3)
    shape = (BANDS, BLOCK, COLS)
    base = jnp.clip(jax.random.normal(base_key, shape, jnp.float32), -6.0, 6.0)
    row_scale = jnp.power(10.0, jax.random.uniform(row_key, (BANDS, BLOCK, 1), jnp.float32) - 0.5)
    col_scale = jnp.power(10.0, jax.random.uniform(col_key, (1, 1, COLS), jnp.float32) - 0.5)
    ramp = (0.5 + jnp.arange(BLOCK, dtype=jnp.float32) / BLOCK).reshape(1, BLOCK, 1)
    return (base * row_scale * col_scale * ramp).astype(jnp.bfloat16)


def draw_left_root(key, part):
    key = jax.random.fold_in(key, 11)
    return root_matrix(key, 0.2)


def draw_right_root(key, part):
    key = jax.random.fold_in(key, 13)
    return root_matrix(key, 0.2)


def draw_block_owner(key, part):
    shared = block_layout(key)
    return shared[2]


def draw_row_offset(key, part):
    shared = block_layout(key)
    return shared[0]


def draw_col_offset(key, part):
    shared = block_layout(key)
    return shared[1]


def block_levels(rng, dims, pieces, least, high):
    def one(axis_at, shards_of):
        draws = jax.random.uniform(jax.random.fold_in(jax.random.fold_in(rng, 6), axis_at), (shards_of,), jnp.float32, least / len(pieces), high / len(pieces))
        return jnp.repeat(jnp.exp(draws), dims[axis_at] // shards_of).reshape((-1,) + (1,) * (len(dims) - axis_at - 1))

    loudness = one(*pieces[0])
    for cut in pieces[1:]:
        loudness = loudness * one(*cut)
    return loudness


def setup_inputs(seed: int = 0) -> dict:
    keys = jax.random.split(jax.random.key(seed), 8)
    return {
        "gradient": draw_gradient(jax.random.fold_in(keys[7], 71), 0),
        "second_moment": jnp.clip(jnp.exp(math.log(5.0) - 4.609084 * jax.random.uniform(keys[1], (BANDS, BLOCK, COLS), jnp.float32) ** block_levels(keys[1], (BANDS, BLOCK, COLS), ((1, 64), (2, 4)), -0.2, 0.2)), 0.049804688, 5.0).astype(jnp.bfloat16),
        "left_root": draw_left_root(jax.random.fold_in(keys[7], 71), 0),
        "right_root": draw_right_root(jax.random.fold_in(keys[7], 71), 0),
        "block_owner": draw_block_owner(jax.random.fold_in(keys[7], 71), 0),
        "row_offset": draw_row_offset(jax.random.fold_in(keys[7], 71), 0),
        "col_offset": draw_col_offset(jax.random.fold_in(keys[7], 71), 0),
    }


def layout_indices(block_owner, row_offset, col_offset):
    block_band = (row_offset // BLOCK).astype(jnp.int32)
    block_col = (col_offset // BLOCK).astype(jnp.int32)
    col_range = (block_col // (COLS // (N_GROUP * BLOCK))).astype(jnp.int32)
    block_count = block_owner.shape[0]
    position = jnp.arange(block_count, dtype=jnp.int32)
    earlier = (col_range[:, None] == col_range[None, :]) & (block_owner[:, None] == block_owner[None, :]) & (position[None, :] < position[:, None])
    slot_index = lax.optimization_barrier(jnp.sum(earlier.astype(jnp.int32), axis=1)).astype(jnp.int32)
    return (block_band, block_col, col_range, slot_index)

def reference(gradient, second_moment, left_root, right_root, block_owner, row_offset, col_offset):
    grad_wide = gradient.astype(jnp.float32)
    new_moment = (0.95 * second_moment.astype(jnp.float32) + 0.05 * grad_wide * grad_wide).astype(jnp.bfloat16)
    adam_dir = grad_wide / (jnp.sqrt(new_moment.astype(jnp.float32)) + 1e-08)
    block_band, block_col, col_range, slot_index = layout_indices(block_owner, row_offset, col_offset)
    block_count = block_owner.shape[0]

    def one_block(block_id):
        band_at = block_band[block_id]
        start = (block_col[block_id] * BLOCK).astype(jnp.int32)
        zero_row = jnp.int32(0)
        grad_tile = lax.dynamic_slice(gradient, (band_at, zero_row, start), (1, BLOCK, BLOCK))[0]
        adam_tile = lax.dynamic_slice(adam_dir, (band_at, zero_row, start), (1, BLOCK, BLOCK))[0]
        left_inv = left_root[block_owner[block_id], col_range[block_id], slot_index[block_id]]
        right_inv = right_root[block_owner[block_id], col_range[block_id], slot_index[block_id]]
        stat_left = jnp.dot(grad_tile, grad_tile.T, preferred_element_type=jnp.float32) / BLOCK
        stat_right = jnp.dot(grad_tile.T, grad_tile, preferred_element_type=jnp.float32) / BLOCK
        half_done = jnp.dot(left_inv, grad_tile, preferred_element_type=jnp.float32).astype(jnp.bfloat16)
        precond = jnp.dot(half_done, right_inv, preferred_element_type=jnp.float32)
        graft_scale = jnp.sqrt(jnp.mean(adam_tile * adam_tile) / (jnp.mean(precond * precond) + 1e-06))
        return (stat_left, stat_right, (precond * graft_scale).astype(jnp.bfloat16))
    stats_left, stats_right, tiles = lax.map(one_block, jnp.arange(block_count, dtype=jnp.int32))
    left_stat = jnp.zeros((N_FSDP, N_GROUP, SLOTS, BLOCK, BLOCK), jnp.float32).at[block_owner, col_range, slot_index].set(stats_left)
    right_stat = jnp.zeros((N_FSDP, N_GROUP, SLOTS, BLOCK, BLOCK), jnp.float32).at[block_owner, col_range, slot_index].set(stats_right)
    tile_grid = jnp.zeros((BANDS, COLS // BLOCK, BLOCK, BLOCK), tiles.dtype).at[block_band, block_col].set(tiles)
    update = tile_grid.transpose(0, 2, 1, 3).reshape(BANDS, BLOCK, COLS)
    return (update, new_moment, left_stat, right_stat)
```

```python
import functools

import jax
import jax.numpy as jnp
from jax import lax
from jax.experimental import pallas as pl
from jax.experimental.pallas import tpu as pltpu
from jax.sharding import PartitionSpec as P

MESH = pl.DeviceIdType.MESH
F32 = jnp.float32
BF16 = jnp.bfloat16

N = 64
X, Z, C = 4, 8, 2
Q = 4
T = 512
BANDS = 16
R = 8
W = 2048
NC = W // T
IN_CHUNKS = 2
OUT_CHUNKS = 4
IW = T // IN_CHUNKS
OW = T // OUT_CHUNKS


def peer(me, k):
    step = k // 8
    half = (step + 1) // 2
    far = jnp.where(step % 2 == 1, half, Z - half)
    dz = lax.rem(4 + far, Z)
    dx = (k // 2 + 2) % X
    dc = k % 2
    c = lax.rem(me, C)
    z = lax.rem(lax.div(me, C), Z)
    x = lax.div(me, C * Z)
    return (lax.rem(x + dx, X) * Z + lax.rem(z + dz, Z)) * C + lax.rem(c + dc, C)


def others(me, fn):
    def one(k, carry):
        d = peer(me, k)
        fn(d)
        return carry

    own = SELF
    lax.fori_loop(0, own, one, 0)
    lax.fori_loop(own + 1, N, one, 0)


def find_self():
    for k in range(N):
        step = k // 8
        half = (step + 1) // 2
        far = half if step % 2 == 1 else Z - half
        if (4 + far) % Z == 0 and (k // 2 + 2) % X == 0 and k % 2 == 0:
            return k


SELF = find_self()


def exchange_kernel(
    idx, g_hbm, m_hbm, l_hbm, r_hbm, y_out, g_out,
    gv, mv, lv, rv, pieces, apart, send_g, recv_g, grad, pre, send_u, ru0, ru1, ru2, ru3, ysrc, send_a, recv_a,
    load_sem, gs, gr, as_, ar, us, ur, ys, yr, keep_sem,
):
    recv_u = (ru0, ru1, ru2, ru3)
    me = lax.axis_index("fsdp")
    mine = lax.axis_index("group")

    barrier = pltpu.get_barrier_semaphore()
    others(me, lambda d: pl.semaphore_signal(barrier, inc=1, device_id={"fsdp": d}, device_id_type=MESH))
    for k in range(1, Q):
        pl.semaphore_signal(
            barrier, inc=1, device_id={"group": lax.rem(mine + k, Q)}, device_id_type=MESH
        )

    loads = [
        pltpu.make_async_copy(src, dst, load_sem.at[i])
        for i, (src, dst) in enumerate([(g_hbm, gv), (m_hbm, mv), (l_hbm, lv), (r_hbm, rv)])
    ]
    for load in loads:
        load.start()
    loads[0].wait()

    def split(b, carry):
        rows = gv[b].astype(F32)
        for c in range(NC):
            pieces[b * NC + c] = rows[:, c * T : (c + 1) * T]
        return carry

    lax.fori_loop(0, BANDS, split, 0)
    pieces[N] = jnp.zeros((R, T), F32)

    def pack(o, carry):
        both = jnp.concatenate([pieces[idx[0, o]], pieces[idx[1, o]]], axis=0)
        send_g[o] = both.astype(BF16)
        return carry

    lax.fori_loop(0, N, pack, 0)

    pl.semaphore_wait(barrier, N - 1 + Q - 1)

    for j in range(IN_CHUNKS):
        cols = pl.ds(j * IW, IW)

        def send(d, cols=cols, j=j):
            pltpu.make_async_remote_copy(
                send_g.at[d, :, cols], recv_g.at[me, :, cols], gs.at[j], gr.at[j],
                device_id={"fsdp": d}, device_id_type=MESH,
            ).start()

        others(me, send)
    recv_g[me] = send_g[me]

    loads[1].wait()

    def adam(b, carry):
        g = gv[b].astype(F32)
        m = mv[b].astype(F32)
        moment = (0.95 * m + 0.05 * g * g).astype(BF16).astype(F32)
        a = g / (jnp.sqrt(moment) + 1e-8)
        sq = a * a
        for c in range(NC):
            part = sq[:, c * T : c * T + 128]
            for i in range(1, T // 128):
                part = part + sq[:, c * T + i * 128 : c * T + (i + 1) * 128]
            apart[b * NC + c] = part
        return carry

    lax.fori_loop(0, BANDS, adam, 0)
    apart[N] = jnp.zeros((R, 128), F32)

    def pack_adam(o, carry):
        first = jnp.sum(apart[idx[0, o]], axis=0, keepdims=True)
        second = jnp.sum(apart[idx[1, o]], axis=0, keepdims=True)
        send_a[o] = jnp.concatenate([first, second], axis=0)
        return carry

    lax.fori_loop(0, N, pack_adam, 0)

    def send_adam(d):
        pltpu.make_async_remote_copy(
            send_a.at[d], recv_a.at[me], as_, ar, device_id={"fsdp": d}, device_id_type=MESH
        ).start()

    others(me, send_adam)
    recv_a[me] = send_a[me]

    loads[2].wait()
    loads[3].wait()

    group_rows = 8
    for j in range(IN_CHUNKS):
        cols = pl.ds(j * IW, IW)
        got = recv_g.at[pl.ds(0, N - 1), :, cols]
        pltpu.make_async_copy(got, got, gr.at[j]).wait()

        def sort(t, carry, cols=cols):
            v = recv_g[pl.ds(t * group_rows, group_rows), :, cols].astype(F32)
            for s in range(2):
                rows = v[:, s * R : (s + 1) * R, :].reshape(group_rows * R, IW)
                grad[s, pl.ds(t * group_rows * R, group_rows * R), cols] = rows.astype(BF16)
            return carry

        lax.fori_loop(0, N // group_rows, sort, 0)
        for s in range(2):
            half = jnp.dot(lv[s], grad[s, :, cols], preferred_element_type=F32).astype(BF16)
            out = jnp.dot(half, rv[s, cols, :], preferred_element_type=F32)
            if j == 0:
                pre[s] = out
            else:
                pre[s] = pre[s] + out

    keep = pltpu.make_async_copy(grad, g_out, keep_sem.at[0])
    keep.start()

    got = recv_a.at[pl.ds(0, N - 1)]
    pltpu.make_async_copy(got, got, ar).wait()
    a_sum = jnp.sum(jnp.sum(recv_a[...], axis=0), axis=1, keepdims=True)
    scale = []
    for s in range(2):
        sq = jnp.sum(pre[s] * pre[s], axis=0, keepdims=True)
        p_mean = jnp.sum(sq, axis=1, keepdims=True) / (T * T)
        scale.append(jnp.sqrt(a_sum[s : s + 1] / (T * T) / (p_mean + 1e-6)))

    for j in range(OUT_CHUNKS):
        cols = pl.ds(j * OW, OW)
        tiles = [(pre[s, :, cols] * scale[s]).reshape(N, R, OW) for s in range(2)]
        send_u[j] = jnp.concatenate(tiles, axis=1).astype(BF16)

        def send(d, j=j):
            pltpu.make_async_remote_copy(
                send_u.at[j, d], recv_u[j].at[me], us.at[j], ur.at[j],
                device_id={"fsdp": d}, device_id_type=MESH,
            ).start()

        others(me, send)
        recv_u[j][me] = send_u[j, me]

    gathers = []
    for j in range(OUT_CHUNKS):
        got = recv_u[j].at[pl.ds(0, N - 1)]
        pltpu.make_async_copy(got, got, ur.at[j]).wait()

        def pick(bp, carry, j=j):
            for c in range(NC):
                rows = []
                for e in range(2):
                    p = (2 * bp + e) * NC + c
                    t = recv_u[j][idx[2, p]].astype(F32)
                    rows.append(jnp.where(idx[3, p] == 0, t[:R], t[R:]))
                ysrc[j, pl.ds(bp * 2 * R, 2 * R), c * OW : (c + 1) * OW] = jnp.concatenate(
                    rows, axis=0
                ).astype(BF16)
            return carry

        lax.fori_loop(0, BANDS // 2, pick, 0)
        for k in (2, 1, 3):
            copy = pltpu.make_async_remote_copy(
                ysrc.at[j], y_out.at[mine, j], ys.at[j, k - 1], yr.at[j, k - 1],
                device_id={"group": lax.rem(mine + k, Q)}, device_id_type=MESH,
            )
            copy.start()
            gathers.append(copy)
        local = pltpu.make_async_copy(ysrc.at[j], y_out.at[mine, j], keep_sem.at[1 + j])
        local.start()
        gathers.append(local)

    keep.wait()
    for copy in gathers:
        copy.wait()
    for j in range(IN_CHUNKS):
        sent = send_g.at[pl.ds(0, N - 1), :, pl.ds(j * IW, IW)]
        pltpu.make_async_copy(sent, sent, gs.at[j]).wait()
    for j in range(OUT_CHUNKS):
        sent = send_u.at[j, pl.ds(0, N - 1)]
        pltpu.make_async_copy(sent, sent, us.at[j]).wait()
    sent = send_a.at[pl.ds(0, N - 1)]
    pltpu.make_async_copy(sent, sent, as_).wait()


def finish_kernel(y, g, m, gr, update, moment, left, right):
    for j in range(OUT_CHUNKS):
        for c in range(NC):
            tile = y[0, j, :, c * OW : (c + 1) * OW].astype(F32).reshape(BANDS, R, OW)
            update[:, :, c * T + j * OW : c * T + (j + 1) * OW] = tile.astype(BF16)
    wide = g[...].astype(F32)
    moment[...] = (0.95 * m[...].astype(F32) + 0.05 * wide * wide).astype(BF16)
    h = lax.rem(pl.program_id(0), 2) * 256
    part = pl.ds(pl.multiple_of(h, 256), 256)
    whole = gr[0]
    left[0, 0, 0] = (
        lax.dot_general(gr[0, part, :], whole, (((1,), (1,)), ((), ())), preferred_element_type=F32) / T
    )
    right[0, 0, 0] = (
        lax.dot_general(gr[0, :, part], whole, (((0,), (0,)), ((), ())), preferred_element_type=F32) / T
    )


def positions(block_owner, row_offset, col_offset):
    col = col_offset // T
    piece = (row_offset // T) * NC + col % NC
    here = (col // NC) == lax.axis_index("group")
    code = jnp.arange(block_owner.shape[0], dtype=jnp.int32) * N + piece
    ids = jnp.arange(N, dtype=jnp.int32)
    match = (block_owner[None, :] == ids[:, None]) & here[None, :]
    first = jnp.min(jnp.where(match, code[None, :], 1 << 20), axis=1)
    last = jnp.max(jnp.where(match, code[None, :], -1), axis=1)
    p0 = jnp.where(last >= 0, first % N, N)
    p1 = jnp.where(last > first, last % N, N)
    is0 = p0[None, :] == ids[:, None]
    is1 = p1[None, :] == ids[:, None]
    owner = jnp.sum(jnp.where(is0 | is1, ids[None, :], 0), axis=1)
    slot = jnp.sum(is1.astype(jnp.int32), axis=1)
    return jnp.stack([p0, p1, owner, slot])


def body(gradient, second_moment, left_root, right_root, block_owner, row_offset, col_offset):
    idx = positions(block_owner, row_offset, col_offset)
    hbm = pl.BlockSpec(memory_space=pl.ANY)
    dma = pltpu.SemaphoreType.DMA
    y_all, grad = pl.pallas_call(
        exchange_kernel,
        out_shape=[
            jax.ShapeDtypeStruct((Q, OUT_CHUNKS, BANDS * R, NC * OW), BF16),
            jax.ShapeDtypeStruct((2, T, T), BF16),
        ],
        in_specs=[pl.BlockSpec(memory_space=pltpu.SMEM), hbm, hbm, hbm, hbm],
        out_specs=[hbm, hbm],
        scratch_shapes=[
            pltpu.VMEM((BANDS, R, W), BF16),
            pltpu.VMEM((BANDS, R, W), BF16),
            pltpu.VMEM((2, T, T), BF16),
            pltpu.VMEM((2, T, T), BF16),
            pltpu.VMEM((N + 1, R, T), F32),
            pltpu.VMEM((N + 1, R, 128), F32),
            pltpu.VMEM((N, 2 * R, T), BF16),
            pltpu.VMEM((N, 2 * R, T), BF16),
            pltpu.VMEM((2, T, T), BF16),
            pltpu.VMEM((2, T, T), F32),
            pltpu.VMEM((OUT_CHUNKS, N, 2 * R, OW), BF16),
            *[pltpu.VMEM((N, 2 * R, OW), BF16)] * OUT_CHUNKS,
            pltpu.VMEM((OUT_CHUNKS, BANDS * R, NC * OW), BF16),
            pltpu.VMEM((N, 2, 128), F32),
            pltpu.VMEM((N, 2, 128), F32),
            dma((4,)),
            dma((IN_CHUNKS,)),
            dma((IN_CHUNKS,)),
            dma,
            dma,
            dma((OUT_CHUNKS,)),
            dma((OUT_CHUNKS,)),
            dma((OUT_CHUNKS, Q - 1)),
            dma((OUT_CHUNKS, Q - 1)),
            dma((1 + OUT_CHUNKS,)),
        ],
        compiler_params=pltpu.CompilerParams(
            collective_id=0, has_side_effects=True, vmem_limit_bytes=60 << 20
        ),
    )(idx, gradient, second_moment, left_root[0, 0], right_root[0, 0])

    steps = 4
    stat = pl.BlockSpec((1, 1, 1, T // 2, T), lambda t: (0, 0, t // 2, t % 2, 0))
    bands = pl.BlockSpec((BANDS // steps, R, W), lambda t: (t, 0, 0))
    update, moment, left, right = pl.pallas_call(
        finish_kernel,
        grid=(steps,),
        out_shape=[
            jax.ShapeDtypeStruct((BANDS, R, Q * W), BF16),
            jax.ShapeDtypeStruct((BANDS, R, W), BF16),
            jax.ShapeDtypeStruct((1, 1, 2, T, T), F32),
            jax.ShapeDtypeStruct((1, 1, 2, T, T), F32),
        ],
        in_specs=[
            pl.BlockSpec((1, OUT_CHUNKS, BANDS * R, NC * OW), lambda t: (t, 0, 0, 0)),
            bands,
            bands,
            pl.BlockSpec((1, T, T), lambda t: (t // 2, 0, 0)),
        ],
        out_specs=[pl.BlockSpec((BANDS, R, W), lambda t: (0, 0, t)), bands, stat, stat],
        compiler_params=pltpu.CompilerParams(vmem_limit_bytes=60 << 20),
    )(y_all, gradient, second_moment, grad)
    return update, moment, left, right


def solution(mesh):
    placed = P(None, "fsdp", "group")
    slots = P("fsdp", "group", None, None, None)
    return jax.shard_map(
        body,
        mesh=mesh,
        in_specs=(placed, placed, slots, slots, P(), P(), P()),
        out_specs=(P(None, "fsdp", None), placed, slots, slots),
        check_vma=False,
    )
```

```python
import functools

import jax
import jax.numpy as jnp
from jax import lax
from jax.experimental import pallas as pl
from jax.experimental.pallas import tpu as pltpu
from jax.sharding import PartitionSpec as P

MESH = pl.DeviceIdType.MESH
F32 = jnp.float32
BF16 = jnp.bfloat16

N = 64
X, Z, C = 4, 8, 2
Q = 4
T = 512
BANDS = 16
R = 8
W = 2048
NC = W // T
IN_CHUNKS = 2
OUT_CHUNKS = 4
IW = T // IN_CHUNKS
OW = T // OUT_CHUNKS


def peer(me, k):
    step = k // 8
    half = (step + 1) // 2
    far = jnp.where(step % 2 == 1, half, Z - half)
    dz = lax.rem(4 + far, Z)
    dx = (k // 2 + 2) % X
    dc = k % 2
    c = lax.rem(me, C)
    z = lax.rem(lax.div(me, C), Z)
    x = lax.div(me, C * Z)
    return (lax.rem(x + dx, X) * Z + lax.rem(z + dz, Z)) * C + lax.rem(c + dc, C)


def others(me, fn):
    def one(k, carry):
        d = peer(me, k)
        fn(d)
        return carry

    own = SELF
    lax.fori_loop(0, own, one, 0)
    lax.fori_loop(own + 1, N, one, 0)


def find_self():
    for k in range(N):
        step = k // 8
        half = (step + 1) // 2
        far = half if step % 2 == 1 else Z - half
        if (4 + far) % Z == 0 and (k // 2 + 2) % X == 0 and k % 2 == 0:
            return k


SELF = find_self()


def exchange_kernel(
    o_hbm, r0_hbm, c0_hbm, g_hbm, m_hbm, l_hbm, r_hbm, y_all, moment, left, right,
    where_v, idx_v, idx, gv, mv, lv, rv, pieces, apart, send_g, recv_g, grad, pre,
    send_u, ru0, ru1, ru2, ru3, send_a, recv_a,
    load_sem, idx_sem, gs, gr, as_, ar, us, ur, ys, yr,
):
    recv_u = (ru0, ru1, ru2, ru3)
    me = lax.axis_index("fsdp")
    mine = lax.axis_index("group")

    loads = [
        pltpu.make_async_copy(src, dst, load_sem.at[i])
        for i, (src, dst) in enumerate(
            [
                (g_hbm, gv), (m_hbm, mv), (l_hbm, lv), (r_hbm, rv),
                (o_hbm, where_v.at[0]), (r0_hbm, where_v.at[1]), (c0_hbm, where_v.at[2]),
            ]
        )
    ]
    for i in (4, 5, 6, 0, 1, 2, 3):
        loads[i].start()

    barrier = pltpu.get_barrier_semaphore()
    others(me, lambda d: pl.semaphore_signal(barrier, inc=1, device_id={"fsdp": d}, device_id_type=MESH))
    for k in range(1, Q):
        pl.semaphore_signal(
            barrier, inc=1, device_id={"group": lax.rem(mine + k, Q)}, device_id_type=MESH
        )

    for i in (4, 5, 6):
        loads[i].wait()
    positions(where_v, idx_v, mine)
    to_smem = pltpu.make_async_copy(idx_v, idx, idx_sem)
    to_smem.start()

    loads[0].wait()

    def split(b, carry):
        rows = gv[b].astype(F32)
        for c in range(NC):
            pieces[b * NC + c] = rows[:, c * T : (c + 1) * T]
        return carry

    lax.fori_loop(0, BANDS, split, 0)
    pieces[N] = jnp.zeros((R, T), F32)
    to_smem.wait()

    def pack(o, carry):
        both = jnp.concatenate([pieces[idx[0, o]], pieces[idx[1, o]]], axis=0)
        send_g[o] = both.astype(BF16)
        return carry

    lax.fori_loop(0, N, pack, 0)

    pl.semaphore_wait(barrier, N - 1 + Q - 1)

    def send_chunk(j):
        cols = pl.ds(j * IW, IW)

        def send(d):
            pltpu.make_async_remote_copy(
                send_g.at[d, :, cols], recv_g.at[me, :, cols], gs.at[j], gr.at[j],
                device_id={"fsdp": d}, device_id_type=MESH,
            ).start()

        others(me, send)

    send_chunk(0)
    recv_g[me] = send_g[me]

    loads[1].wait()

    def adam(b, carry):
        g = gv[b].astype(F32)
        m = mv[b].astype(F32)
        second = (0.95 * m + 0.05 * g * g).astype(BF16)
        moment[b] = second
        a = g / (jnp.sqrt(second.astype(F32)) + 1e-8)
        sq = a * a
        for c in range(NC):
            part = sq[:, c * T : c * T + 128]
            for i in range(1, T // 128):
                part = part + sq[:, c * T + i * 128 : c * T + (i + 1) * 128]
            apart[b * NC + c] = part
        return carry

    lax.fori_loop(0, BANDS, adam, 0)
    apart[N] = jnp.zeros((R, 128), F32)

    def pack_adam(o, carry):
        first = jnp.sum(apart[idx[0, o]], axis=0, keepdims=True)
        second = jnp.sum(apart[idx[1, o]], axis=0, keepdims=True)
        send_a[o] = jnp.concatenate([first, second], axis=0)
        return carry

    lax.fori_loop(0, N, pack_adam, 0)

    def send_adam(d):
        pltpu.make_async_remote_copy(
            send_a.at[d], recv_a.at[me], as_, ar, device_id={"fsdp": d}, device_id_type=MESH
        ).start()

    others(me, send_adam)
    for j in range(1, IN_CHUNKS):
        send_chunk(j)
    recv_a[me] = send_a[me]

    loads[2].wait()
    loads[3].wait()

    group_rows = 8
    for j in range(IN_CHUNKS):
        cols = pl.ds(j * IW, IW)
        got = recv_g.at[pl.ds(0, N - 1), :, cols]
        pltpu.make_async_copy(got, got, gr.at[j]).wait()

        def sort(t, carry, cols=cols):
            v = recv_g[pl.ds(t * group_rows, group_rows), :, cols].astype(F32)
            for s in range(2):
                rows = v[:, s * R : (s + 1) * R, :].reshape(group_rows * R, IW)
                grad[s, pl.ds(t * group_rows * R, group_rows * R), cols] = rows.astype(BF16)
            return carry

        lax.fori_loop(0, N // group_rows, sort, 0)
        for s in range(2):
            half = jnp.dot(lv[s], grad[s, :, cols], preferred_element_type=F32).astype(BF16)
            out = jnp.dot(half, rv[s, cols, :], preferred_element_type=F32)
            if j == 0:
                pre[s] = out
            else:
                pre[s] = pre[s] + out

    got = recv_a.at[pl.ds(0, N - 1)]
    pltpu.make_async_copy(got, got, ar).wait()
    a_sum = jnp.sum(jnp.sum(recv_a[...], axis=0), axis=1, keepdims=True)
    scale = []
    for s in range(2):
        sq = jnp.sum(pre[s] * pre[s], axis=0, keepdims=True)
        p_mean = jnp.sum(sq, axis=1, keepdims=True) / (T * T)
        scale.append(jnp.sqrt(a_sum[s : s + 1] / (T * T) / (p_mean + 1e-6)))

    for j in range(OUT_CHUNKS):
        cols = pl.ds(j * OW, OW)
        tiles = [(pre[s, :, cols] * scale[s]).reshape(N, R, OW) for s in range(2)]
        send_u[j] = jnp.concatenate(tiles, axis=1).astype(BF16)

        def send(d, j=j):
            pltpu.make_async_remote_copy(
                send_u.at[j, d], recv_u[j].at[me], us.at[j], ur.at[j],
                device_id={"fsdp": d}, device_id_type=MESH,
            ).start()

        others(me, send)
        recv_u[j][me] = send_u[j, me]

    for s in range(2):
        g = grad[s]
        left[s] = (
            lax.dot_general(g, g, (((1,), (1,)), ((), ())), preferred_element_type=F32) / T
        )
        right[s] = (
            lax.dot_general(g, g, (((0,), (0,)), ((), ())), preferred_element_type=F32) / T
        )

    gathers = []
    for j in range(OUT_CHUNKS):
        got = recv_u[j].at[pl.ds(0, N - 1)]
        pltpu.make_async_copy(got, got, ur.at[j]).wait()

        def pick(b, carry, j=j):
            for c in range(NC):
                p = b * NC + c
                t = recv_u[j][idx[2, p]].astype(F32)
                rows = jnp.where(idx[3, p] == 0, t[:R], t[R:])
                y_all[mine, j, b, :, c * OW : (c + 1) * OW] = rows.astype(BF16)
            return carry

        lax.fori_loop(0, BANDS, pick, 0)
        for k in (2, 1, 3):
            copy = pltpu.make_async_remote_copy(
                y_all.at[mine, j], y_all.at[mine, j], ys.at[j, k - 1], yr.at[j, k - 1],
                device_id={"group": lax.rem(mine + k, Q)}, device_id_type=MESH,
            )
            copy.start()
            gathers.append(copy)

    for copy in gathers:
        copy.wait()
    for j in range(IN_CHUNKS):
        sent = send_g.at[pl.ds(0, N - 1), :, pl.ds(j * IW, IW)]
        pltpu.make_async_copy(sent, sent, gs.at[j]).wait()
    for j in range(OUT_CHUNKS):
        sent = send_u.at[j, pl.ds(0, N - 1)]
        pltpu.make_async_copy(sent, sent, us.at[j]).wait()
    sent = send_a.at[pl.ds(0, N - 1)]
    pltpu.make_async_copy(sent, sent, as_).wait()


def finish_kernel(y_all, moment, left, right, update_out, moment_out, left_out, right_out, sem):
    copies = [
        pltpu.make_async_copy(left, left_out.at[0, 0], sem.at[0]),
        pltpu.make_async_copy(right, right_out.at[0, 0], sem.at[1]),
        pltpu.make_async_copy(moment, moment_out, sem.at[2]),
    ]
    for q in range(Q):
        for j in range(OUT_CHUNKS):
            for c in range(NC):
                copies.append(
                    pltpu.make_async_copy(
                        y_all.at[q, j, :, :, pl.ds(c * OW, OW)],
                        update_out.at[:, :, pl.ds(q * W + c * T + j * OW, OW)],
                        sem.at[len(copies)],
                    )
                )
    for copy in copies:
        copy.start()
    for copy in copies:
        copy.wait()


def positions(where_v, out, mine):
    owner, row, col = where_v[0], where_v[1], where_v[2]
    blocks = owner.shape[1]
    col = col // T
    piece = (row // T) * NC + col % NC
    here = (col // NC) == mine
    code = lax.broadcasted_iota(jnp.int32, (1, blocks), 1) * N + piece
    owner = jnp.where(here, owner, N)
    match = owner == lax.broadcasted_iota(jnp.int32, (N, blocks), 0)
    first = jnp.min(jnp.where(match, code, 1 << 20), axis=1, keepdims=True)
    last = jnp.max(jnp.where(match, code, -1), axis=1, keepdims=True)
    p0 = jnp.where(last >= 0, first % N, N)
    p1 = jnp.where(last > first, last % N, N)
    sub = lax.broadcasted_iota(jnp.int32, (N, 128), 0)
    lane = lax.broadcasted_iota(jnp.int32, (N, 128), 1)
    own_lane = sub == lane
    is0, is1 = p0 == lane, p1 == lane

    def total(v):
        return jnp.sum(v, axis=0, keepdims=True)

    out[0:1] = total(jnp.where(own_lane, p0, 0))
    out[1:2] = total(jnp.where(own_lane, p1, 0))
    out[2:3] = total(jnp.where(is0 | is1, sub, 0))
    out[3:4] = total(jnp.where(is1, 1, 0))


def body(gradient, second_moment, left_root, right_root, block_owner, row_offset, col_offset):
    hbm = pl.BlockSpec(memory_space=pltpu.HBM)
    vmem = pl.BlockSpec(memory_space=pltpu.VMEM)
    dma = pltpu.SemaphoreType.DMA
    blocks = block_owner.shape[0]
    places = [v.reshape(1, blocks) for v in (block_owner, row_offset, col_offset)]
    operands = [
        pltpu.with_memory_space_constraint(v, pltpu.HBM)
        for v in (*places, gradient, second_moment, left_root[0, 0], right_root[0, 0])
    ]
    kept = pl.pallas_call(
        exchange_kernel,
        out_shape=[
            pltpu.VMEM((Q, OUT_CHUNKS, BANDS, R, NC * OW), BF16),
            pltpu.VMEM((BANDS, R, W), BF16),
            pltpu.VMEM((2, T, T), F32),
            pltpu.VMEM((2, T, T), F32),
        ],
        in_specs=[hbm] * 7,
        out_specs=[vmem] * 4,
        scratch_shapes=[
            pltpu.VMEM((3, 1, blocks), jnp.int32),
            pltpu.VMEM((8, 128), jnp.int32),
            pltpu.SMEM((8, 128), jnp.int32),
            pltpu.VMEM((BANDS, R, W), BF16),
            pltpu.VMEM((BANDS, R, W), BF16),
            pltpu.VMEM((2, T, T), BF16),
            pltpu.VMEM((2, T, T), BF16),
            pltpu.VMEM((N + 1, R, T), F32),
            pltpu.VMEM((N + 1, R, 128), F32),
            pltpu.VMEM((N, 2 * R, T), BF16),
            pltpu.VMEM((N, 2 * R, T), BF16),
            pltpu.VMEM((2, T, T), BF16),
            pltpu.VMEM((2, T, T), F32),
            pltpu.VMEM((OUT_CHUNKS, N, 2 * R, OW), BF16),
            *[pltpu.VMEM((N, 2 * R, OW), BF16)] * OUT_CHUNKS,
            pltpu.VMEM((N, 2, 128), F32),
            pltpu.VMEM((N, 2, 128), F32),
            dma((7,)),
            dma,
            dma((IN_CHUNKS,)),
            dma((IN_CHUNKS,)),
            dma,
            dma,
            dma((OUT_CHUNKS,)),
            dma((OUT_CHUNKS,)),
            dma((OUT_CHUNKS, Q - 1)),
            dma((OUT_CHUNKS, Q - 1)),
        ],
        compiler_params=pltpu.CompilerParams(
            collective_id=0, has_side_effects=True, vmem_limit_bytes=32 << 20
        ),
    )(*operands)

    return pl.pallas_call(
        finish_kernel,
        out_shape=[
            jax.ShapeDtypeStruct((BANDS, R, Q * W), BF16),
            jax.ShapeDtypeStruct((BANDS, R, W), BF16),
            jax.ShapeDtypeStruct((1, 1, 2, T, T), F32),
            jax.ShapeDtypeStruct((1, 1, 2, T, T), F32),
        ],
        in_specs=[vmem] * 4,
        out_specs=[hbm] * 4,
        scratch_shapes=[dma((3 + Q * OUT_CHUNKS * NC,))],
        compiler_params=pltpu.CompilerParams(vmem_limit_bytes=16 << 20),
    )(*kept)


def solution(mesh):
    placed = P(None, "fsdp", "group")
    slots = P("fsdp", "group", None, None, None)
    return jax.shard_map(
        body,
        mesh=mesh,
        in_specs=(placed, placed, slots, slots, P(), P(), P()),
        out_specs=(P(None, "fsdp", None), placed, slots, slots),
        check_vma=False,
    )
```

```python
import functools

import jax
import jax.numpy as jnp
from jax import lax
from jax.experimental import pallas as pl
from jax.experimental.pallas import tpu as pltpu
from jax.sharding import PartitionSpec as P

MESH = pl.DeviceIdType.MESH
F32 = jnp.float32
BF16 = jnp.bfloat16

N = 64
X, Z, C = 4, 8, 2
Q = 4
T = 512
BANDS = 16
R = 8
W = 2048
NC = W // T
IN_CHUNKS = 2
OUT_CHUNKS = 4
IW = T // IN_CHUNKS
OW = T // OUT_CHUNKS


def others(me, fn):
    c = lax.rem(me, C)
    z = lax.rem(lax.div(me, C), Z)
    x = lax.div(me, C * Z)
    near = [
        lax.rem(x + dx, X) * (Z * C) + lax.rem(c + dc, C)
        for dx, dc in ((2, 0), (2, 1), (1, 0), (1, 1), (3, 0), (3, 1), (0, 1), (0, 0))
    ]

    def far(k, carry):
        half = (k + 1) // 2
        dz = jnp.where(k % 2 == 1, half, Z - half)
        row = lax.rem(z + 4 + dz, Z) * C
        for there in near:
            fn(there + row)
        return carry

    lax.fori_loop(0, Z - 1, far, 0)
    for there in near[:-1]:
        fn(there + z * C)


def exchange_kernel(
    o_hbm, r0_hbm, c0_hbm, g_hbm, m_hbm, l_hbm, r_hbm, y_all, moment, left, right,
    where_v, idx_v, idx, gv, mv, lv, rv, pieces, apart, send_g, recv_g, grad, pre,
    send_u, ru0, ru1, ru2, ru3, send_a, recv_a,
    load_sem, idx_sem, gs, gr, as_, ar, us, ur, ys, yr,
):
    recv_u = (ru0, ru1, ru2, ru3)
    me = lax.axis_index("fsdp")
    mine = lax.axis_index("group")

    loads = [
        pltpu.make_async_copy(src, dst, load_sem.at[i])
        for i, (src, dst) in enumerate(
            [
                (g_hbm, gv), (m_hbm, mv), (l_hbm, lv), (r_hbm, rv),
                (o_hbm, where_v.at[0]), (r0_hbm, where_v.at[1]), (c0_hbm, where_v.at[2]),
            ]
        )
    ]
    for i in (4, 5, 6, 0, 1, 2, 3):
        loads[i].start()

    barrier = pltpu.get_barrier_semaphore()
    others(me, lambda d: pl.semaphore_signal(barrier, inc=1, device_id={"fsdp": d}, device_id_type=MESH))
    for k in range(1, Q):
        pl.semaphore_signal(
            barrier, inc=1, device_id={"group": lax.rem(mine + k, Q)}, device_id_type=MESH
        )

    for i in (4, 5, 6):
        loads[i].wait()
    positions(where_v, idx_v, mine)
    to_smem = pltpu.make_async_copy(idx_v, idx, idx_sem)
    to_smem.start()

    loads[0].wait()

    def split(b, carry):
        rows = gv[b].astype(F32)
        for c in range(NC):
            pieces[b * NC + c] = rows[:, c * T : (c + 1) * T]
        return carry

    lax.fori_loop(0, BANDS, split, 0)
    pieces[N] = jnp.zeros((R, T), F32)
    to_smem.wait()

    def pack(o, carry):
        both = jnp.concatenate([pieces[idx[0, o]], pieces[idx[1, o]]], axis=0)
        send_g[o] = both.astype(BF16)
        return carry

    lax.fori_loop(0, N, pack, 0)

    pl.semaphore_wait(barrier, N - 1 + Q - 1)

    def send_chunk(j):
        cols = pl.ds(j * IW, IW)

        def send(d):
            pltpu.make_async_remote_copy(
                send_g.at[d, :, cols], recv_g.at[me, :, cols], gs.at[j], gr.at[j],
                device_id={"fsdp": d}, device_id_type=MESH,
            ).start()

        others(me, send)

    send_chunk(0)
    recv_g[me] = send_g[me]

    loads[1].wait()

    def adam(b, carry):
        g = gv[b].astype(F32)
        m = mv[b].astype(F32)
        second = (0.95 * m + 0.05 * g * g).astype(BF16)
        moment[b] = second
        a = g / (jnp.sqrt(second.astype(F32)) + 1e-8)
        sq = a * a
        for c in range(NC):
            part = sq[:, c * T : c * T + 128]
            for i in range(1, T // 128):
                part = part + sq[:, c * T + i * 128 : c * T + (i + 1) * 128]
            apart[b * NC + c] = part
        return carry

    lax.fori_loop(0, BANDS, adam, 0)
    apart[N] = jnp.zeros((R, 128), F32)

    def pack_adam(o, carry):
        first = jnp.sum(apart[idx[0, o]], axis=0, keepdims=True)
        second = jnp.sum(apart[idx[1, o]], axis=0, keepdims=True)
        send_a[o] = jnp.concatenate([first, second], axis=0)
        return carry

    lax.fori_loop(0, N, pack_adam, 0)

    def send_adam(d):
        pltpu.make_async_remote_copy(
            send_a.at[d], recv_a.at[me], as_, ar, device_id={"fsdp": d}, device_id_type=MESH
        ).start()

    others(me, send_adam)
    for j in range(1, IN_CHUNKS):
        send_chunk(j)
    recv_a[me] = send_a[me]

    loads[2].wait()
    loads[3].wait()

    group_rows = 8
    for j in range(IN_CHUNKS):
        cols = pl.ds(j * IW, IW)
        got = recv_g.at[pl.ds(0, N - 1), :, cols]
        pltpu.make_async_copy(got, got, gr.at[j]).wait()

        def sort(t, carry, cols=cols):
            v = recv_g[pl.ds(t * group_rows, group_rows), :, cols].astype(F32)
            for s in range(2):
                rows = v[:, s * R : (s + 1) * R, :].reshape(group_rows * R, IW)
                grad[s, pl.ds(t * group_rows * R, group_rows * R), cols] = rows.astype(BF16)
            return carry

        lax.fori_loop(0, N // group_rows, sort, 0)
        for s in range(2):
            half = jnp.dot(lv[s], grad[s, :, cols], preferred_element_type=F32).astype(BF16)
            out = jnp.dot(half, rv[s, cols, :], preferred_element_type=F32)
            if j == 0:
                pre[s] = out
            else:
                pre[s] = pre[s] + out

    got = recv_a.at[pl.ds(0, N - 1)]
    pltpu.make_async_copy(got, got, ar).wait()
    a_sum = jnp.sum(jnp.sum(recv_a[...], axis=0), axis=1, keepdims=True)
    scale = []
    for s in range(2):
        sq = jnp.sum(pre[s] * pre[s], axis=0, keepdims=True)
        p_mean = jnp.sum(sq, axis=1, keepdims=True) / (T * T)
        scale.append(jnp.sqrt(a_sum[s : s + 1] / (T * T) / (p_mean + 1e-6)))

    for j in range(OUT_CHUNKS):
        cols = pl.ds(j * OW, OW)
        tiles = [(pre[s, :, cols] * scale[s]).reshape(N, R, OW) for s in range(2)]
        send_u[j] = jnp.concatenate(tiles, axis=1).astype(BF16)

        def send(d, j=j):
            pltpu.make_async_remote_copy(
                send_u.at[j, d], recv_u[j].at[me], us.at[j], ur.at[j],
                device_id={"fsdp": d}, device_id_type=MESH,
            ).start()

        others(me, send)
        recv_u[j][me] = send_u[j, me]

    for s in range(2):
        g = grad[s]
        left[s] = (
            lax.dot_general(g, g, (((1,), (1,)), ((), ())), preferred_element_type=F32) / T
        )
        right[s] = (
            lax.dot_general(g, g, (((0,), (0,)), ((), ())), preferred_element_type=F32) / T
        )

    gathers = []
    for j in range(OUT_CHUNKS):
        got = recv_u[j].at[pl.ds(0, N - 1)]
        pltpu.make_async_copy(got, got, ur.at[j]).wait()

        def pick(b, carry, j=j):
            for c in range(NC):
                p = b * NC + c
                t = recv_u[j][idx[2, p]].astype(F32)
                rows = jnp.where(idx[3, p] == 0, t[:R], t[R:])
                y_all[mine, j, b, :, c * OW : (c + 1) * OW] = rows.astype(BF16)
            return carry

        lax.fori_loop(0, BANDS, pick, 0)
        for k in (2, 1, 3):
            copy = pltpu.make_async_remote_copy(
                y_all.at[mine, j], y_all.at[mine, j], ys.at[j, k - 1], yr.at[j, k - 1],
                device_id={"group": lax.rem(mine + k, Q)}, device_id_type=MESH,
            )
            copy.start()
            gathers.append(copy)

    for copy in gathers:
        copy.wait()
    for j in range(IN_CHUNKS):
        sent = send_g.at[pl.ds(0, N - 1), :, pl.ds(j * IW, IW)]
        pltpu.make_async_copy(sent, sent, gs.at[j]).wait()
    for j in range(OUT_CHUNKS):
        sent = send_u.at[j, pl.ds(0, N - 1)]
        pltpu.make_async_copy(sent, sent, us.at[j]).wait()
    sent = send_a.at[pl.ds(0, N - 1)]
    pltpu.make_async_copy(sent, sent, as_).wait()


def finish_kernel(y_all, moment, left, right, update_out, moment_out, left_out, right_out, sem):
    copies = [
        pltpu.make_async_copy(left, left_out.at[0, 0], sem.at[0]),
        pltpu.make_async_copy(right, right_out.at[0, 0], sem.at[1]),
        pltpu.make_async_copy(moment, moment_out, sem.at[2]),
    ]
    for q in range(Q):
        for j in range(OUT_CHUNKS):
            for c in range(NC):
                copies.append(
                    pltpu.make_async_copy(
                        y_all.at[q, j, :, :, pl.ds(c * OW, OW)],
                        update_out.at[:, :, pl.ds(q * W + c * T + j * OW, OW)],
                        sem.at[len(copies)],
                    )
                )
    for copy in copies:
        copy.start()
    for copy in copies:
        copy.wait()


def positions(where_v, out, mine):
    owner, row, col = where_v[0], where_v[1], where_v[2]
    blocks = owner.shape[1]
    col = col // T
    piece = (row // T) * NC + col % NC
    here = (col // NC) == mine
    code = lax.broadcasted_iota(jnp.int32, (1, blocks), 1) * N + piece
    owner = jnp.where(here, owner, N)
    match = owner == lax.broadcasted_iota(jnp.int32, (N, blocks), 0)
    first = jnp.min(jnp.where(match, code, 1 << 20), axis=1, keepdims=True)
    last = jnp.max(jnp.where(match, code, -1), axis=1, keepdims=True)
    p0 = jnp.where(last >= 0, first % N, N)
    p1 = jnp.where(last > first, last % N, N)
    sub = lax.broadcasted_iota(jnp.int32, (N, 128), 0)
    lane = lax.broadcasted_iota(jnp.int32, (N, 128), 1)
    own_lane = sub == lane
    is0, is1 = p0 == lane, p1 == lane

    def total(v):
        return jnp.sum(v, axis=0, keepdims=True)

    out[0:1] = total(jnp.where(own_lane, p0, 0))
    out[1:2] = total(jnp.where(own_lane, p1, 0))
    out[2:3] = total(jnp.where(is0 | is1, sub, 0))
    out[3:4] = total(jnp.where(is1, 1, 0))


def body(gradient, second_moment, left_root, right_root, block_owner, row_offset, col_offset):
    hbm = pl.BlockSpec(memory_space=pltpu.HBM)
    vmem = pl.BlockSpec(memory_space=pltpu.VMEM)
    dma = pltpu.SemaphoreType.DMA
    blocks = block_owner.shape[0]
    places = [v.reshape(1, blocks) for v in (block_owner, row_offset, col_offset)]
    operands = [
        pltpu.with_memory_space_constraint(v, pltpu.HBM)
        for v in (*places, gradient, second_moment, left_root[0, 0], right_root[0, 0])
    ]
    kept = pl.pallas_call(
        exchange_kernel,
        out_shape=[
            pltpu.VMEM((Q, OUT_CHUNKS, BANDS, R, NC * OW), BF16),
            pltpu.VMEM((BANDS, R, W), BF16),
            pltpu.VMEM((2, T, T), F32),
            pltpu.VMEM((2, T, T), F32),
        ],
        in_specs=[hbm] * 7,
        out_specs=[vmem] * 4,
        scratch_shapes=[
            pltpu.VMEM((3, 1, blocks), jnp.int32),
            pltpu.VMEM((8, 128), jnp.int32),
            pltpu.SMEM((8, 128), jnp.int32),
            pltpu.VMEM((BANDS, R, W), BF16),
            pltpu.VMEM((BANDS, R, W), BF16),
            pltpu.VMEM((2, T, T), BF16),
            pltpu.VMEM((2, T, T), BF16),
            pltpu.VMEM((N + 1, R, T), F32),
            pltpu.VMEM((N + 1, R, 128), F32),
            pltpu.VMEM((N, 2 * R, T), BF16),
            pltpu.VMEM((N, 2 * R, T), BF16),
            pltpu.VMEM((2, T, T), BF16),
            pltpu.VMEM((2, T, T), F32),
            pltpu.VMEM((OUT_CHUNKS, N, 2 * R, OW), BF16),
            *[pltpu.VMEM((N, 2 * R, OW), BF16)] * OUT_CHUNKS,
            pltpu.VMEM((N, 2, 128), F32),
            pltpu.VMEM((N, 2, 128), F32),
            dma((7,)),
            dma,
            dma((IN_CHUNKS,)),
            dma((IN_CHUNKS,)),
            dma,
            dma,
            dma((OUT_CHUNKS,)),
            dma((OUT_CHUNKS,)),
            dma((OUT_CHUNKS, Q - 1)),
            dma((OUT_CHUNKS, Q - 1)),
        ],
        compiler_params=pltpu.CompilerParams(
            collective_id=0, has_side_effects=True, vmem_limit_bytes=32 << 20
        ),
    )(*operands)

    return pl.pallas_call(
        finish_kernel,
        out_shape=[
            jax.ShapeDtypeStruct((BANDS, R, Q * W), BF16),
            jax.ShapeDtypeStruct((BANDS, R, W), BF16),
            jax.ShapeDtypeStruct((1, 1, 2, T, T), F32),
            jax.ShapeDtypeStruct((1, 1, 2, T, T), F32),
        ],
        in_specs=[vmem] * 4,
        out_specs=[hbm] * 4,
        scratch_shapes=[dma((3 + Q * OUT_CHUNKS * NC,))],
        compiler_params=pltpu.CompilerParams(vmem_limit_bytes=16 << 20),
    )(*kept)


def solution(mesh):
    placed = P(None, "fsdp", "group")
    slots = P("fsdp", "group", None, None, None)
    return jax.shard_map(
        body,
        mesh=mesh,
        in_specs=(placed, placed, slots, slots, P(), P(), P()),
        out_specs=(P(None, "fsdp", None), placed, slots, slots),
        check_vma=False,
    )
```

```python
import functools

import jax
import jax.numpy as jnp
from jax import lax
from jax.experimental import pallas as pl
from jax.experimental.pallas import tpu as pltpu
from jax.sharding import PartitionSpec as P

MESH = pl.DeviceIdType.MESH
F32 = jnp.float32
BF16 = jnp.bfloat16

N = 64
X, Z, C = 4, 8, 2
Q = 4
T = 512
BANDS = 16
R = 8
W = 2048
NC = W // T
HW = T // 2
OUT_CHUNKS = 4
SINGLE = N - N // 4
STEP_BANDS = 2


def place(me):
    return lax.div(me, C * Z), lax.rem(lax.div(me, C), Z), lax.rem(me, C)


def near(me):
    x, _, c = place(me)
    return [
        lax.rem(x + dx, X) * (Z * C) + lax.rem(c + dc, C)
        for dx, dc in ((2, 0), (2, 1), (1, 0), (1, 1), (3, 0), (3, 1), (0, 1), (0, 0))
    ]


def others_far(me, fn, first, last):
    z = place(me)[1]
    same = near(me)

    def far(k, carry):
        half = (k + 1) // 2
        dz = jnp.where(k % 2 == 1, half, Z - half)
        row = lax.rem(z + 4 + dz, Z) * C
        for there in same:
            fn(there + row)
        return carry

    lax.fori_loop(first, last, far, 0)


def others_near(me, fn):
    z = place(me)[1]
    for there in near(me)[:-1]:
        fn(there + z * C)


def others(me, fn):
    others_far(me, fn, 0, Z - 1)
    others_near(me, fn)


def exchange_kernel(
    o_hbm, r0_hbm, c0_hbm, g_hbm, m_hbm, l_hbm, r_hbm, y_all, moment, left, right, table,
    where_v, idx_v, idx, gv, mv, lv, rv, pieces, apart, send_g, recv_g, grad, pre,
    send_u, ru0, ru1, ru2, ru3, sum_a, recv_a, sum_b, recv_b,
    load_sem, idx_sem, gs, gr, as_, ar, bs, br, us, ur, ys, yr,
):
    recv_u = (ru0, ru1, ru2, ru3)
    me = lax.axis_index("fsdp")
    mine = lax.axis_index("group")
    x, z, core = place(me)
    spot = x * C + core

    loads = [
        pltpu.make_async_copy(src, dst, load_sem.at[i])
        for i, (src, dst) in enumerate(
            [
                (g_hbm, gv), (m_hbm, mv), (l_hbm, lv), (r_hbm, rv),
                (o_hbm, where_v.at[0]), (r0_hbm, where_v.at[1]), (c0_hbm, where_v.at[2]),
            ]
        )
    ]
    for i in (4, 5, 6, 0, 1, 2, 3):
        loads[i].start()

    barrier = pltpu.get_barrier_semaphore()
    others(me, lambda d: pl.semaphore_signal(barrier, inc=1, device_id={"fsdp": d}, device_id_type=MESH))
    for k in range(1, Q):
        pl.semaphore_signal(
            barrier, inc=1, device_id={"group": lax.rem(mine + k, Q)}, device_id_type=MESH
        )

    for i in (4, 5, 6):
        loads[i].wait()
    row0, row1, owners, _ = positions(where_v, mine)
    idx_v[0:1] = row0
    idx_v[1:2] = row1
    idx_v[2:3] = owners
    to_smem = pltpu.make_async_copy(idx_v, idx, idx_sem)
    to_smem.start()

    loads[0].wait()

    def split(b, carry):
        rows = gv[b].astype(F32)
        for c in range(NC):
            for h in range(2):
                at = c * T + h * HW
                pieces[b * NC + c, h * R : (h + 1) * R] = rows[:, at : at + HW]
        return carry

    lax.fori_loop(0, BANDS, split, 0)
    pieces[N] = jnp.zeros((2 * R, HW), F32)
    to_smem.wait()

    def pack(o, carry):
        for s in range(2):
            send_g[s, o] = pieces[idx[s, o]].astype(BF16)
        return carry

    lax.fori_loop(0, N, pack, 0)

    pl.semaphore_wait(barrier, N - 1 + Q - 1)

    def send_slot(s):
        def send(d):
            pltpu.make_async_remote_copy(
                send_g.at[s, d], recv_g.at[s, me], gs.at[s], gr.at[s],
                device_id={"fsdp": d}, device_id_type=MESH,
            ).start()

        return send

    others(me, send_slot(0))

    loads[1].wait()

    def adam(b, carry):
        g = gv[b].astype(F32)
        m = mv[b].astype(F32)
        second = (0.95 * m + 0.05 * g * g).astype(BF16)
        moment[b] = second
        a = g / (jnp.sqrt(second.astype(F32)) + 1e-8)
        sq = a * a
        for c in range(NC):
            part = sq[:, c * T : c * T + 128]
            for i in range(1, T // 128):
                part = part + sq[:, c * T + i * 128 : c * T + (i + 1) * 128]
            apart[b * NC + c] = part
        return carry

    lax.fori_loop(0, BANDS, adam, 0)
    column = jnp.sum(jnp.sum(apart[...], axis=1), axis=1, keepdims=True)
    own_lane = lax.broadcasted_iota(jnp.int32, (N, 128), 0) == lax.broadcasted_iota(
        jnp.int32, (N, 128), 1
    )
    sum_a[...] = jnp.sum(jnp.where(own_lane, column, 0.0), axis=0, keepdims=True)
    recv_a[z] = sum_a[...]
    for dz in range(1, Z):
        pltpu.make_async_remote_copy(
            sum_a, recv_a.at[z], as_, ar,
            device_id={"fsdp": x * (Z * C) + lax.rem(z + dz, Z) * C + core}, device_id_type=MESH,
        ).start()
    others_far(me, send_slot(1), 0, 3)
    got = recv_a.at[pl.ds(0, Z - 1)]
    pltpu.make_async_copy(got, got, ar).wait()
    sum_b[...] = jnp.sum(recv_a[...], axis=0)
    recv_b[spot] = sum_b[...]

    def send_b(d):
        pltpu.make_async_remote_copy(
            sum_b, recv_b.at[spot], bs, br, device_id={"fsdp": d}, device_id_type=MESH
        ).start()

    others_near(me, send_b)
    others_far(me, send_slot(1), 3, Z - 1)
    others_near(me, send_slot(1))
    for s in range(2):
        recv_g[s, me] = send_g[s, me]

    loads[2].wait()
    loads[3].wait()

    group_rows = 8
    for s in range(2):
        got = recv_g.at[s, pl.ds(0, N - 1)]
        pltpu.make_async_copy(got, got, gr.at[s]).wait()

        def sort(t, carry, s=s):
            v = recv_g[s, pl.ds(t * group_rows, group_rows)].astype(F32)
            for h in range(2):
                rows = v[:, h * R : (h + 1) * R, :].reshape(group_rows * R, HW)
                grad[s, pl.ds(t * group_rows * R, group_rows * R), h * HW : (h + 1) * HW] = rows.astype(
                    BF16
                )
            return carry

        lax.fori_loop(0, N // group_rows, sort, 0)
        half = jnp.dot(lv[s], grad[s], preferred_element_type=F32).astype(BF16)
        pre[s] = jnp.dot(half, rv[s], preferred_element_type=F32)

        if s == 0:
            got = recv_b.at[pl.ds(0, X * C - 1)]
            pltpu.make_async_copy(got, got, br).wait()
            adam_sums = jnp.sum(recv_b[...], axis=0)
        lane = lax.broadcasted_iota(jnp.int32, (1, 128), 1)
        a_sum = jnp.sum(jnp.where(lane == idx[s, me], adam_sums, 0.0), axis=1, keepdims=True)
        sq = jnp.sum(pre[s] * pre[s], axis=0, keepdims=True)
        p_mean = jnp.sum(sq, axis=1, keepdims=True) / (T * T)
        scale = jnp.sqrt(a_sum / (T * T) / (p_mean + 1e-6))

        for h in range(2):
            j = s * 2 + h
            tiles = [
                (pre[s, :, pl.ds(h * HW + i * 128, 128)] * scale).reshape(N, R, 128) for i in range(2)
            ]
            send_u[j] = jnp.concatenate(tiles, axis=1).astype(BF16)

            def send(d, j=j):
                pltpu.make_async_remote_copy(
                    send_u.at[j, d], recv_u[j].at[me], us.at[j], ur.at[j],
                    device_id={"fsdp": d}, device_id_type=MESH,
                ).start()

            others(me, send)
            recv_u[j][me] = send_u[j, me]

    for s in range(2):
        g = grad[s]
        left[s] = (
            lax.dot_general(g, g, (((1,), (1,)), ((), ())), preferred_element_type=F32) / T
        )
        right[s] = (
            lax.dot_general(g, g, (((0,), (0,)), ((), ())), preferred_element_type=F32) / T
        )
    for q in range(Q):
        table[q : q + 1] = positions(where_v, q)[3]

    gathers = []
    for s, lo, hi in ((0, 0, SINGLE), (1, SINGLE, N)):
        for h in range(2):
            j = s * 2 + h
            got = recv_u[j].at[pl.ds(0, N - 1)]
            pltpu.make_async_copy(got, got, ur.at[j]).wait()

            def pick(k, carry, j=j, h=h, lo=lo):
                for e in range(4):
                    at = lo + k * 4 + e
                    t = recv_u[j][idx[2, at]].astype(F32)
                    y_all[mine, h, at] = jnp.concatenate([t[:R], t[R:]], axis=1).astype(BF16)
                return carry

            lax.fori_loop(0, (hi - lo) // 4, pick, 0)
            part = y_all.at[mine, h, pl.ds(lo, hi - lo)]
            for k in (2, 1, 3):
                copy = pltpu.make_async_remote_copy(
                    part, part, ys.at[j, k - 1], yr.at[j, k - 1],
                    device_id={"group": lax.rem(mine + k, Q)}, device_id_type=MESH,
                )
                copy.start()
                gathers.append(copy)

    for copy in gathers:
        copy.wait()
    for s in range(2):
        sent = send_g.at[s, pl.ds(0, N - 1)]
        pltpu.make_async_copy(sent, sent, gs.at[s]).wait()
    for j in range(OUT_CHUNKS):
        sent = send_u.at[j, pl.ds(0, N - 1)]
        pltpu.make_async_copy(sent, sent, us.at[j]).wait()
    sent = recv_a.at[pl.ds(0, Z - 1)]
    pltpu.make_async_copy(sent, sent, as_).wait()
    sent = recv_b.at[pl.ds(0, X * C - 1)]
    pltpu.make_async_copy(sent, sent, bs).wait()


def finish_kernel(
    y_all, moment, left, right, table, update_out, moment_out, left_out, right_out, rank, sem
):
    step = pl.program_id(0)
    copies = [
        pltpu.make_async_copy(left, left_out.at[0, 0], sem.at[0]),
        pltpu.make_async_copy(right, right_out.at[0, 0], sem.at[1]),
        pltpu.make_async_copy(moment, moment_out, sem.at[2]),
    ]

    @pl.when(step == 0)
    def _():
        ranks = pltpu.make_async_copy(table, rank, sem.at[3])
        ranks.start()
        for copy in copies:
            copy.start()
        ranks.wait()

    for b in range(STEP_BANDS):
        for q in range(Q):
            for c in range(NC):
                at = rank[q, (step * STEP_BANDS + b) * NC + c]
                for h in range(2):
                    col = q * W + c * T + h * HW
                    update_out[b, :, col : col + HW] = y_all[q, h, at]

    @pl.when(step == BANDS // STEP_BANDS - 1)
    def _():
        for copy in copies:
            copy.wait()


def positions(where_v, q):
    owner, row, col = where_v[0], where_v[1], where_v[2]
    blocks = owner.shape[1]
    col = col // T
    piece = (row // T) * NC + col % NC
    here = (col // NC) == q
    code = lax.broadcasted_iota(jnp.int32, (1, blocks), 1) * N + piece
    owner = jnp.where(here, owner, N)
    match = owner == lax.broadcasted_iota(jnp.int32, (N, blocks), 0)
    first = jnp.min(jnp.where(match, code, 1 << 20), axis=1, keepdims=True)
    last = jnp.max(jnp.where(match, code, -1), axis=1, keepdims=True)
    has0 = last >= 0
    has1 = last > first
    p0 = jnp.where(has0, first % N, N)
    p1 = jnp.where(has1, last % N, N)
    sub = lax.broadcasted_iota(jnp.int32, (N, 128), 0)
    lane = lax.broadcasted_iota(jnp.int32, (N, 128), 1)

    def total(v):
        return jnp.sum(v, axis=0, keepdims=True)

    row0 = total(jnp.where(sub == lane, p0, 0))
    row1 = total(jnp.where(sub == lane, p1, 0))

    def before(row):
        return jnp.sum(jnp.where((lane < sub) & (row < N), 1, 0), axis=1, keepdims=True)

    rank0 = jnp.where(has0, before(row0), -1)
    rank1 = jnp.where(has1, SINGLE + before(row1), -1)
    owners = total(jnp.where((rank0 == lane) | (rank1 == lane), sub, 0))
    ranks = total(jnp.where(p0 == lane, rank0, 0) + jnp.where(p1 == lane, rank1, 0))
    return row0, row1, owners, ranks


def body(gradient, second_moment, left_root, right_root, block_owner, row_offset, col_offset):
    hbm = pl.BlockSpec(memory_space=pltpu.HBM)
    vmem = pl.BlockSpec(memory_space=pltpu.VMEM)
    dma = pltpu.SemaphoreType.DMA
    blocks = block_owner.shape[0]
    places = [v.reshape(1, blocks) for v in (block_owner, row_offset, col_offset)]
    operands = [
        pltpu.with_memory_space_constraint(v, pltpu.HBM)
        for v in (*places, gradient, second_moment, left_root[0, 0], right_root[0, 0])
    ]
    kept = pl.pallas_call(
        exchange_kernel,
        out_shape=[
            pltpu.VMEM((Q, 2, N, R, HW), BF16),
            pltpu.VMEM((BANDS, R, W), BF16),
            pltpu.VMEM((2, T, T), F32),
            pltpu.VMEM((2, T, T), F32),
            pltpu.VMEM((8, 128), jnp.int32),
        ],
        in_specs=[hbm] * 7,
        out_specs=[vmem] * 5,
        scratch_shapes=[
            pltpu.VMEM((3, 1, blocks), jnp.int32),
            pltpu.VMEM((8, 128), jnp.int32),
            pltpu.SMEM((8, 128), jnp.int32),
            pltpu.VMEM((BANDS, R, W), BF16),
            pltpu.VMEM((BANDS, R, W), BF16),
            pltpu.VMEM((2, T, T), BF16),
            pltpu.VMEM((2, T, T), BF16),
            pltpu.VMEM((N + 1, 2 * R, HW), F32),
            pltpu.VMEM((N, R, 128), F32),
            pltpu.VMEM((2, N, 2 * R, HW), BF16),
            pltpu.VMEM((2, N, 2 * R, HW), BF16),
            pltpu.VMEM((2, T, T), BF16),
            pltpu.VMEM((2, T, T), F32),
            pltpu.VMEM((OUT_CHUNKS, N, 2 * R, 128), BF16),
            *[pltpu.VMEM((N, 2 * R, 128), BF16)] * OUT_CHUNKS,
            pltpu.VMEM((1, 128), F32),
            pltpu.VMEM((Z, 1, 128), F32),
            pltpu.VMEM((1, 128), F32),
            pltpu.VMEM((X * C, 1, 128), F32),
            dma((7,)),
            dma,
            dma((2,)),
            dma((2,)),
            dma,
            dma,
            dma,
            dma,
            dma((OUT_CHUNKS,)),
            dma((OUT_CHUNKS,)),
            dma((OUT_CHUNKS, Q - 1)),
            dma((OUT_CHUNKS, Q - 1)),
        ],
        compiler_params=pltpu.CompilerParams(
            collective_id=0, has_side_effects=True, vmem_limit_bytes=32 << 20
        ),
    )(*operands)

    return pl.pallas_call(
        finish_kernel,
        grid=(BANDS // STEP_BANDS,),
        out_shape=[
            jax.ShapeDtypeStruct((BANDS, R, Q * W), BF16),
            jax.ShapeDtypeStruct((BANDS, R, W), BF16),
            jax.ShapeDtypeStruct((1, 1, 2, T, T), F32),
            jax.ShapeDtypeStruct((1, 1, 2, T, T), F32),
        ],
        in_specs=[vmem] * 5,
        out_specs=[pl.BlockSpec((STEP_BANDS, R, Q * W), lambda t: (t, 0, 0)), hbm, hbm, hbm],
        scratch_shapes=[pltpu.SMEM((8, 128), jnp.int32), dma((4,))],
        compiler_params=pltpu.CompilerParams(vmem_limit_bytes=16 << 20),
    )(*kept)


def solution(mesh):
    placed = P(None, "fsdp", "group")
    slots = P("fsdp", "group", None, None, None)
    return jax.shard_map(
        body,
        mesh=mesh,
        in_specs=(placed, placed, slots, slots, P(), P(), P()),
        out_specs=(P(None, "fsdp", None), placed, slots, slots),
        check_vma=False,
    )
```

```python
import functools

import jax
import jax.numpy as jnp
from jax import lax
from jax.experimental import pallas as pl
from jax.experimental.pallas import tpu as pltpu
from jax.sharding import PartitionSpec as P

MESH = pl.DeviceIdType.MESH
F32 = jnp.float32
BF16 = jnp.bfloat16

N = 64
X, Z, C = 4, 8, 2
Q = 4
T = 512
BANDS = 16
R = 8
W = 2048
NC = W // T
HW = T // 2
OUT_CHUNKS = 4
SINGLE = N - N // 4
STEP_BANDS = 4


def place(me):
    return lax.div(me, C * Z), lax.rem(lax.div(me, C), Z), lax.rem(me, C)


def near(me):
    x, _, c = place(me)
    return [
        lax.rem(x + dx, X) * (Z * C) + lax.rem(c + dc, C)
        for dx, dc in ((2, 0), (2, 1), (1, 0), (1, 1), (3, 0), (3, 1), (0, 1), (0, 0))
    ]


def others_far(me, fn, first, last):
    z = place(me)[1]
    same = near(me)

    def far(k, carry):
        half = (k + 1) // 2
        dz = jnp.where(k % 2 == 1, half, Z - half)
        row = lax.rem(z + 4 + dz, Z) * C
        for there in same:
            fn(there + row)
        return carry

    lax.fori_loop(first, last, far, 0)


def others_near(me, fn):
    z = place(me)[1]
    for there in near(me)[:-1]:
        fn(there + z * C)


def others(me, fn):
    others_far(me, fn, 0, Z - 1)
    others_near(me, fn)


def exchange_kernel(
    o_hbm, r0_hbm, c0_hbm, g_hbm, m_hbm, l_hbm, r_hbm, y_all, moment, left, right, table,
    where_v, idx_v, idx, table_v, gv, mv, lv, rv, pieces, apart, send_g, recv_g, grad, pre,
    send_u, ru0, ru1, ru2, ru3, sum_a, recv_a, sum_b, recv_b,
    load_sem, idx_sem, gs, gr, as_, ar, bs, br, us, ur, ys, yr,
):
    recv_u = (ru0, ru1, ru2, ru3)
    me = lax.axis_index("fsdp")
    mine = lax.axis_index("group")
    x, z, core = place(me)
    spot = x * C + core

    loads = [
        pltpu.make_async_copy(src, dst, load_sem.at[i])
        for i, (src, dst) in enumerate(
            [
                (g_hbm, gv), (m_hbm, mv), (l_hbm, lv), (r_hbm, rv),
                (o_hbm, where_v.at[0]), (r0_hbm, where_v.at[1]), (c0_hbm, where_v.at[2]),
            ]
        )
    ]
    for i in (4, 5, 6, 0, 1, 2, 3):
        loads[i].start()

    barrier = pltpu.get_barrier_semaphore()

    def greet(d):
        pl.semaphore_signal(barrier, inc=1, device_id={"fsdp": d}, device_id_type=MESH)

    others_far(me, greet, 0, 4)
    for k in range(1, Q):
        pl.semaphore_signal(
            barrier, inc=1, device_id={"group": lax.rem(mine + k, Q)}, device_id_type=MESH
        )

    for i in (4, 5, 6):
        loads[i].wait()
    row0, row1, _, _ = positions(where_v, mine)
    idx_v[0:1] = row0
    idx_v[1:2] = row1
    to_smem = pltpu.make_async_copy(idx_v, idx, idx_sem)
    to_smem.start()
    others_far(me, greet, 4, Z - 1)
    others_near(me, greet)

    loads[0].wait()

    def split(b, carry):
        rows = gv[b].astype(F32)
        for c in range(NC):
            for h in range(2):
                at = c * T + h * HW
                pieces[b * NC + c, h * R : (h + 1) * R] = rows[:, at : at + HW]
        return carry

    lax.fori_loop(0, BANDS, split, 0)
    pieces[N] = jnp.zeros((2 * R, HW), F32)
    to_smem.wait()

    def pack(s):
        def four(k, carry):
            for e in range(4):
                o = k * 4 + e
                send_g[s, o] = pieces[idx[s, o]].astype(BF16)
            return carry

        lax.fori_loop(0, N // 4, four, 0)

    pack(0)

    pl.semaphore_wait(barrier, N - 1 + Q - 1)

    def send_slot(s):
        def send(d):
            pltpu.make_async_remote_copy(
                send_g.at[s, d], recv_g.at[s, me], gs.at[s], gr.at[s],
                device_id={"fsdp": d}, device_id_type=MESH,
            ).start()

        return send

    others(me, send_slot(0))
    pack(1)

    loads[1].wait()

    def adam(b, carry):
        g = gv[b].astype(F32)
        m = mv[b].astype(F32)
        second = (0.95 * m + 0.05 * g * g).astype(BF16)
        moment[b] = second
        a = g / (jnp.sqrt(second.astype(F32)) + 1e-8)
        sq = a * a
        for c in range(NC):
            part = sq[:, c * T : c * T + 128]
            for i in range(1, T // 128):
                part = part + sq[:, c * T + i * 128 : c * T + (i + 1) * 128]
            apart[b * NC + c] = part
        return carry

    lax.fori_loop(0, BANDS, adam, 0)
    column = jnp.sum(jnp.sum(apart[...], axis=1), axis=1, keepdims=True)
    own_lane = lax.broadcasted_iota(jnp.int32, (N, 128), 0) == lax.broadcasted_iota(
        jnp.int32, (N, 128), 1
    )
    sum_a[...] = jnp.sum(jnp.where(own_lane, column, 0.0), axis=0, keepdims=True)
    recv_a[z] = sum_a[...]
    for dz in range(1, Z):
        pltpu.make_async_remote_copy(
            sum_a, recv_a.at[z], as_, ar,
            device_id={"fsdp": x * (Z * C) + lax.rem(z + dz, Z) * C + core}, device_id_type=MESH,
        ).start()
    others_far(me, send_slot(1), 0, 3)
    got = recv_a.at[pl.ds(0, Z - 1)]
    pltpu.make_async_copy(got, got, ar).wait()
    sum_b[...] = jnp.sum(recv_a[...], axis=0)
    recv_b[spot] = sum_b[...]

    def send_b(d):
        pltpu.make_async_remote_copy(
            sum_b, recv_b.at[spot], bs, br, device_id={"fsdp": d}, device_id_type=MESH
        ).start()

    others_near(me, send_b)
    others_far(me, send_slot(1), 3, Z - 1)
    others_near(me, send_slot(1))
    for s in range(2):
        recv_g[s, me] = send_g[s, me]

    loads[2].wait()
    loads[3].wait()

    group_rows = 8
    for s in range(2):
        got = recv_g.at[s, pl.ds(0, N - 1)]
        pltpu.make_async_copy(got, got, gr.at[s]).wait()

        def sort(t, carry, s=s):
            v = recv_g[s, pl.ds(t * group_rows, group_rows)].astype(F32)
            for h in range(2):
                rows = v[:, h * R : (h + 1) * R, :].reshape(group_rows * R, HW)
                grad[s, pl.ds(t * group_rows * R, group_rows * R), h * HW : (h + 1) * HW] = rows.astype(
                    BF16
                )
            return carry

        lax.fori_loop(0, N // group_rows, sort, 0)
        half = jnp.dot(lv[s], grad[s], preferred_element_type=F32).astype(BF16)
        pre[s] = jnp.dot(half, rv[s], preferred_element_type=F32)

        if s == 0:
            got = recv_b.at[pl.ds(0, X * C - 1)]
            pltpu.make_async_copy(got, got, br).wait()
            adam_sums = jnp.sum(recv_b[...], axis=0)
        lane = lax.broadcasted_iota(jnp.int32, (1, 128), 1)
        a_sum = jnp.sum(jnp.where(lane == idx[s, me], adam_sums, 0.0), axis=1, keepdims=True)
        sq = jnp.sum(pre[s] * pre[s], axis=0, keepdims=True)
        p_mean = jnp.sum(sq, axis=1, keepdims=True) / (T * T)
        scale = jnp.sqrt(a_sum / (T * T) / (p_mean + 1e-6))

        for h in range(2):
            j = s * 2 + h
            tiles = [
                (pre[s, :, pl.ds(h * HW + i * 128, 128)] * scale).reshape(N, R, 128) for i in range(2)
            ]
            send_u[j] = jnp.concatenate(tiles, axis=1).astype(BF16)

            def send(d, j=j):
                pltpu.make_async_remote_copy(
                    send_u.at[j, d], recv_u[j].at[me], us.at[j], ur.at[j],
                    device_id={"fsdp": d}, device_id_type=MESH,
                ).start()

            others(me, send)
            recv_u[j][me] = send_u[j, me]

    for s in range(2):
        g = grad[s]
        left[s] = (
            lax.dot_general(g, g, (((1,), (1,)), ((), ())), preferred_element_type=F32) / T
        )
        right[s] = (
            lax.dot_general(g, g, (((0,), (0,)), ((), ())), preferred_element_type=F32) / T
        )
    for q in range(Q):
        table_v[q : q + 1] = positions(where_v, q)[3]
    table_v[Q : Q + 1] = positions(where_v, mine)[2]
    to_table = pltpu.make_async_copy(table_v, table, idx_sem)
    to_table.start()
    to_table.wait()

    gathers = []
    relays = []

    def send_y(part, j, way, k):
        copy = pltpu.make_async_remote_copy(
            part, part, ys.at[j, way], yr.at[j, way],
            device_id={"group": lax.rem(mine + k, Q)}, device_id_type=MESH,
        )
        copy.start()
        return copy

    def forward():
        for j, h, right_copy, left_copy in relays:
            right_copy.wait_recv()
            gathers.append(send_y(y_all.at[lax.rem(mine + 3, Q), h, pl.ds(0, SINGLE // 2)], j, 2, 1))
            left_copy.wait_recv()
            gathers.append(
                send_y(y_all.at[lax.rem(mine + 1, Q), h, pl.ds(SINGLE // 2, SINGLE // 2)], j, 3, 3)
            )
            right_copy.wait_send()
            left_copy.wait_send()
        relays.clear()

    for s, lo, hi in ((0, 0, SINGLE), (1, SINGLE, N)):
        for h in range(2):
            j = s * 2 + h
            got = recv_u[j].at[pl.ds(0, N - 1)]
            pltpu.make_async_copy(got, got, ur.at[j]).wait()

            def pick(k, carry, j=j, h=h, lo=lo):
                for e in range(4):
                    at = lo + k * 4 + e
                    t = recv_u[j][table[Q, at]].astype(F32)
                    y_all[mine, h, at] = jnp.concatenate([t[:R], t[R:]], axis=1).astype(BF16)
                return carry

            lax.fori_loop(0, (hi - lo) // 4, pick, 0)
            part = y_all.at[mine, h, pl.ds(lo, hi - lo)]
            if s == 0:
                forward()
                relays.append((j, h, send_y(part, j, 0, 1), send_y(part, j, 1, 3)))
            else:
                if h == 0:
                    forward()
                gathers.extend(send_y(part, j, way, k) for way, k in enumerate((2, 1, 3)))

    for copy in gathers:
        copy.wait()
    for s in range(2):
        sent = send_g.at[s, pl.ds(0, N - 1)]
        pltpu.make_async_copy(sent, sent, gs.at[s]).wait()
    for j in range(OUT_CHUNKS):
        sent = send_u.at[j, pl.ds(0, N - 1)]
        pltpu.make_async_copy(sent, sent, us.at[j]).wait()
    sent = recv_a.at[pl.ds(0, Z - 1)]
    pltpu.make_async_copy(sent, sent, as_).wait()
    sent = recv_b.at[pl.ds(0, X * C - 1)]
    pltpu.make_async_copy(sent, sent, bs).wait()


def finish_kernel(
    y_all, moment, left, right, rank, update_out, moment_out, left_out, right_out, sem
):
    step = pl.program_id(0)
    copies = [
        pltpu.make_async_copy(left, left_out.at[0, 0], sem.at[0]),
        pltpu.make_async_copy(right, right_out.at[0, 0], sem.at[1]),
        pltpu.make_async_copy(moment, moment_out, sem.at[2]),
    ]

    @pl.when(step == 0)
    def _():
        for copy in copies:
            copy.start()

    for b in range(STEP_BANDS):
        for q in range(Q):
            for c in range(NC):
                at = rank[q, (step * STEP_BANDS + b) * NC + c]
                for h in range(2):
                    col = q * W + c * T + h * HW
                    update_out[b, :, col : col + HW] = y_all[q, h, at]

    @pl.when(step == BANDS // STEP_BANDS - 1)
    def _():
        for copy in copies:
            copy.wait()


def positions(where_v, q):
    owner, row, col = where_v[0], where_v[1], where_v[2]
    blocks = owner.shape[1]
    col = col // T
    piece = (row // T) * NC + col % NC
    here = (col // NC) == q
    code = lax.broadcasted_iota(jnp.int32, (1, blocks), 1) * N + piece
    owner = jnp.where(here, owner, N)
    match = owner == lax.broadcasted_iota(jnp.int32, (N, blocks), 0)
    first = jnp.min(jnp.where(match, code, 1 << 20), axis=1, keepdims=True)
    last = jnp.max(jnp.where(match, code, -1), axis=1, keepdims=True)
    has0 = last >= 0
    has1 = last > first
    p0 = jnp.where(has0, first % N, N)
    p1 = jnp.where(has1, last % N, N)
    sub = lax.broadcasted_iota(jnp.int32, (N, 128), 0)
    lane = lax.broadcasted_iota(jnp.int32, (N, 128), 1)

    def total(v):
        return jnp.sum(v, axis=0, keepdims=True)

    row0 = total(jnp.where(sub == lane, p0, 0))
    row1 = total(jnp.where(sub == lane, p1, 0))

    def before(row):
        return jnp.sum(jnp.where((lane < sub) & (row < N), 1, 0), axis=1, keepdims=True)

    rank0 = jnp.where(has0, before(row0), -1)
    rank1 = jnp.where(has1, SINGLE + before(row1), -1)
    owners = total(jnp.where((rank0 == lane) | (rank1 == lane), sub, 0))
    ranks = total(jnp.where(p0 == lane, rank0, 0) + jnp.where(p1 == lane, rank1, 0))
    return row0, row1, owners, ranks


def body(gradient, second_moment, left_root, right_root, block_owner, row_offset, col_offset):
    hbm = pl.BlockSpec(memory_space=pltpu.HBM)
    vmem = pl.BlockSpec(memory_space=pltpu.VMEM)
    smem = pl.BlockSpec(memory_space=pltpu.SMEM)
    dma = pltpu.SemaphoreType.DMA
    blocks = block_owner.shape[0]
    places = [v.reshape(1, blocks) for v in (block_owner, row_offset, col_offset)]
    operands = [
        pltpu.with_memory_space_constraint(v, pltpu.HBM)
        for v in (*places, gradient, second_moment, left_root[0, 0], right_root[0, 0])
    ]
    kept = pl.pallas_call(
        exchange_kernel,
        out_shape=[
            pltpu.VMEM((Q, 2, N, R, HW), BF16),
            pltpu.VMEM((BANDS, R, W), BF16),
            pltpu.VMEM((2, T, T), F32),
            pltpu.VMEM((2, T, T), F32),
            pltpu.SMEM((8, 128), jnp.int32),
        ],
        in_specs=[hbm] * 7,
        out_specs=[vmem] * 4 + [smem],
        scratch_shapes=[
            pltpu.VMEM((3, 1, blocks), jnp.int32),
            pltpu.VMEM((8, 128), jnp.int32),
            pltpu.SMEM((8, 128), jnp.int32),
            pltpu.VMEM((8, 128), jnp.int32),
            pltpu.VMEM((BANDS, R, W), BF16),
            pltpu.VMEM((BANDS, R, W), BF16),
            pltpu.VMEM((2, T, T), BF16),
            pltpu.VMEM((2, T, T), BF16),
            pltpu.VMEM((N + 1, 2 * R, HW), F32),
            pltpu.VMEM((N, R, 128), F32),
            pltpu.VMEM((2, N, 2 * R, HW), BF16),
            pltpu.VMEM((2, N, 2 * R, HW), BF16),
            pltpu.VMEM((2, T, T), BF16),
            pltpu.VMEM((2, T, T), F32),
            pltpu.VMEM((OUT_CHUNKS, N, 2 * R, 128), BF16),
            *[pltpu.VMEM((N, 2 * R, 128), BF16)] * OUT_CHUNKS,
            pltpu.VMEM((1, 128), F32),
            pltpu.VMEM((Z, 1, 128), F32),
            pltpu.VMEM((1, 128), F32),
            pltpu.VMEM((X * C, 1, 128), F32),
            dma((7,)),
            dma,
            dma((2,)),
            dma((2,)),
            dma,
            dma,
            dma,
            dma,
            dma((OUT_CHUNKS,)),
            dma((OUT_CHUNKS,)),
            dma((OUT_CHUNKS, Q)),
            dma((OUT_CHUNKS, Q)),
        ],
        compiler_params=pltpu.CompilerParams(
            collective_id=0, has_side_effects=True, vmem_limit_bytes=32 << 20
        ),
    )(*operands)

    return pl.pallas_call(
        finish_kernel,
        grid=(BANDS // STEP_BANDS,),
        out_shape=[
            jax.ShapeDtypeStruct((BANDS, R, Q * W), BF16),
            jax.ShapeDtypeStruct((BANDS, R, W), BF16),
            jax.ShapeDtypeStruct((1, 1, 2, T, T), F32),
            jax.ShapeDtypeStruct((1, 1, 2, T, T), F32),
        ],
        in_specs=[vmem] * 4 + [smem],
        out_specs=[pl.BlockSpec((STEP_BANDS, R, Q * W), lambda t: (t, 0, 0)), hbm, hbm, hbm],
        scratch_shapes=[dma((3,))],
        compiler_params=pltpu.CompilerParams(vmem_limit_bytes=16 << 20),
    )(*kept)


def solution(mesh):
    placed = P(None, "fsdp", "group")
    slots = P("fsdp", "group", None, None, None)
    return jax.shard_map(
        body,
        mesh=mesh,
        in_specs=(placed, placed, slots, slots, P(), P(), P()),
        out_specs=(P(None, "fsdp", None), placed, slots, slots),
        check_vma=False,
    )
```

```python
import functools

import jax
import jax.numpy as jnp
from jax import lax
from jax.experimental import pallas as pl
from jax.experimental.pallas import tpu as pltpu
from jax.sharding import PartitionSpec as P

MESH = pl.DeviceIdType.MESH
F32 = jnp.float32
BF16 = jnp.bfloat16

N = 64
X, Z, C = 4, 8, 2
Q = 4
T = 512
BANDS = 16
R = 8
W = 2048
NC = W // T
HW = T // 2
OUT_CHUNKS = 4
SINGLE = N - N // 4
STEP_BANDS = 8
EARLY = 7


def place(me):
    return lax.div(me, C * Z), lax.rem(lax.div(me, C), Z), lax.rem(me, C)


def near(me):
    x, _, c = place(me)
    return [
        lax.rem(x + dx, X) * (Z * C) + lax.rem(c + dc, C)
        for dx, dc in ((2, 0), (2, 1), (1, 0), (1, 1), (3, 0), (3, 1), (0, 1), (0, 0))
    ]


def others_far(me, fn, first, last):
    z = place(me)[1]
    same = near(me)

    def far(k, carry):
        half = (k + 1) // 2
        dz = jnp.where(k % 2 == 1, half, Z - half)
        row = lax.rem(z + 4 + dz, Z) * C
        for there in same:
            fn(there + row)
        return carry

    lax.fori_loop(first, last, far, 0)


def others_near(me, fn):
    z = place(me)[1]
    for there in near(me)[:-1]:
        fn(there + z * C)


def others(me, fn):
    others_far(me, fn, 0, Z - 1)
    others_near(me, fn)


def exchange_kernel(
    o_hbm, r0_hbm, c0_hbm, g_hbm, m_hbm, l_hbm, r_hbm, y_all, moment, left, right, table,
    where_v, idx_v, idx, table_v, gv, mv, lv, rv, pieces, apart, send_g, recv_g, grad, pre,
    send_u, ru0, ru1, ru2, ru3, sum_a, recv_a, sum_b, recv_b,
    load_sem, idx_sem, gs, gr, as_, ar, bs, br, us, ur, ys, yr,
):
    recv_u = (ru0, ru1, ru2, ru3)
    me = lax.axis_index("fsdp")
    mine = lax.axis_index("group")
    x, z, core = place(me)
    spot = x * C + core

    loads = [
        pltpu.make_async_copy(src, dst, load_sem.at[i])
        for i, (src, dst) in enumerate(
            [
                (g_hbm, gv), (m_hbm, mv), (l_hbm, lv), (r_hbm, rv),
                (o_hbm, where_v.at[0]), (r0_hbm, where_v.at[1]), (c0_hbm, where_v.at[2]),
            ]
        )
    ]
    for i in (4, 5, 6, 0, 1, 2, 3):
        loads[i].start()

    barrier = pltpu.get_barrier_semaphore()

    def greet(d):
        pl.semaphore_signal(barrier, inc=1, device_id={"fsdp": d}, device_id_type=MESH)

    others_far(me, greet, 0, 4)
    for k in range(1, Q):
        pl.semaphore_signal(
            barrier, inc=1, device_id={"group": lax.rem(mine + k, Q)}, device_id_type=MESH
        )

    for i in (4, 5, 6):
        loads[i].wait()
    row0, row1, _, _ = positions(where_v, mine)
    idx_v[0:1] = row0
    idx_v[1:2] = row1
    to_smem = pltpu.make_async_copy(idx_v, idx, idx_sem)
    to_smem.start()
    others_far(me, greet, 4, Z - 1)
    others_near(me, greet)

    loads[0].wait()

    def split(b, carry):
        rows = gv[b].astype(F32)
        for c in range(NC):
            for h in range(2):
                at = c * T + h * HW
                pieces[b * NC + c, h * R : (h + 1) * R] = rows[:, at : at + HW]
        return carry

    lax.fori_loop(0, BANDS, split, 0)
    pieces[N] = jnp.zeros((2 * R, HW), F32)
    to_smem.wait()

    def pack(s):
        def four(k, carry):
            for e in range(4):
                o = k * 4 + e
                send_g[s, o] = pieces[idx[s, o]].astype(BF16)
            return carry

        lax.fori_loop(0, N // 4, four, 0)

    pack(0)

    pl.semaphore_wait(barrier, N - 1 + Q - 1)

    def send_slot(s):
        def send(d):
            pltpu.make_async_remote_copy(
                send_g.at[s, d], recv_g.at[s, me], gs.at[s], gr.at[s],
                device_id={"fsdp": d}, device_id_type=MESH,
            ).start()

        return send

    others(me, send_slot(0))
    pack(1)

    loads[1].wait()

    def adam(b, carry):
        g = gv[b].astype(F32)
        m = mv[b].astype(F32)
        second = (0.95 * m + 0.05 * g * g).astype(BF16)
        moment[b] = second
        a = g / (jnp.sqrt(second.astype(F32)) + 1e-8)
        sq = a * a
        for c in range(NC):
            part = sq[:, c * T : c * T + 128]
            for i in range(1, T // 128):
                part = part + sq[:, c * T + i * 128 : c * T + (i + 1) * 128]
            apart[b * NC + c] = part
        return carry

    lax.fori_loop(0, BANDS, adam, 0)
    column = jnp.sum(jnp.sum(apart[...], axis=1), axis=1, keepdims=True)
    own_lane = lax.broadcasted_iota(jnp.int32, (N, 128), 0) == lax.broadcasted_iota(
        jnp.int32, (N, 128), 1
    )
    sum_a[...] = jnp.sum(jnp.where(own_lane, column, 0.0), axis=0, keepdims=True)
    recv_a[z] = sum_a[...]
    for dz in range(1, Z):
        pltpu.make_async_remote_copy(
            sum_a, recv_a.at[z], as_, ar,
            device_id={"fsdp": x * (Z * C) + lax.rem(z + dz, Z) * C + core}, device_id_type=MESH,
        ).start()
    others_far(me, send_slot(1), 0, 4)
    got = recv_a.at[pl.ds(0, Z - 1)]
    pltpu.make_async_copy(got, got, ar).wait()
    sum_b[...] = jnp.sum(recv_a[...], axis=0)
    recv_b[spot] = sum_b[...]

    def send_b(d):
        pltpu.make_async_remote_copy(
            sum_b, recv_b.at[spot], bs, br, device_id={"fsdp": d}, device_id_type=MESH
        ).start()

    others_near(me, send_b)
    others_far(me, send_slot(1), 4, Z - 1)
    others_near(me, send_slot(1))
    for q in range(Q):
        table_v[q : q + 1] = positions(where_v, q)[3]
    table_v[Q : Q + 1] = positions(where_v, mine)[2]
    to_table = pltpu.make_async_copy(table_v, table, idx_sem)
    to_table.start()
    to_table.wait()

    for s in range(2):
        recv_g[s, me] = send_g[s, me]

    loads[2].wait()
    loads[3].wait()

    group_rows = 8

    def take(s):
        got = recv_g.at[s, pl.ds(0, N - 1)]
        pltpu.make_async_copy(got, got, gr.at[s]).wait()

        def sort(t, carry):
            v = recv_g[s, pl.ds(t * group_rows, group_rows)].astype(F32)
            for h in range(2):
                rows = v[:, h * R : (h + 1) * R, :].reshape(group_rows * R, HW)
                grad[s, pl.ds(t * group_rows * R, group_rows * R), h * HW : (h + 1) * HW] = rows.astype(
                    BF16
                )
            return carry

        lax.fori_loop(0, N // group_rows, sort, 0)
        half = jnp.dot(lv[s], grad[s], preferred_element_type=F32).astype(BF16)
        pre[s] = jnp.dot(half, rv[s], preferred_element_type=F32)

    def graft(s, adam_sums):
        lane = lax.broadcasted_iota(jnp.int32, (1, 128), 1)
        a_sum = jnp.sum(jnp.where(lane == idx[s, me], adam_sums, 0.0), axis=1, keepdims=True)
        sq = jnp.sum(pre[s] * pre[s], axis=0, keepdims=True)
        p_mean = jnp.sum(sq, axis=1, keepdims=True) / (T * T)
        return jnp.sqrt(a_sum / (T * T) / (p_mean + 1e-6))

    def send_back(s, h, scale):
        j = s * 2 + h
        tiles = [
            (pre[s, :, pl.ds(h * HW + i * 128, 128)] * scale).reshape(N, R, 128) for i in range(2)
        ]
        send_u[j] = jnp.concatenate(tiles, axis=1).astype(BF16)

        def send(d):
            pltpu.make_async_remote_copy(
                send_u.at[j, d], recv_u[j].at[me], us.at[j], ur.at[j],
                device_id={"fsdp": d}, device_id_type=MESH,
            ).start()

        others(me, send)
        recv_u[j][me] = send_u[j, me]

    gathers = []
    relays = []

    def send_y(part, j, way, k):
        copy = pltpu.make_async_remote_copy(
            part, part, ys.at[j, way], yr.at[j, way],
            device_id={"group": lax.rem(mine + k, Q)}, device_id_type=MESH,
        )
        copy.start()
        return copy

    def forward():
        for j, h, right_copy, left_copy in relays:
            right_copy.wait_recv()
            gathers.append(send_y(y_all.at[lax.rem(mine + 3, Q), h, pl.ds(0, SINGLE // 2)], j, 2, 1))
            left_copy.wait_recv()
            gathers.append(
                send_y(y_all.at[lax.rem(mine + 1, Q), h, pl.ds(SINGLE // 2, SINGLE // 2)], j, 3, 3)
            )
            right_copy.wait_send()
            left_copy.wait_send()
        relays.clear()

    def gather(s, h):
        j = s * 2 + h
        lo, hi = (0, SINGLE) if s == 0 else (SINGLE, N)
        got = recv_u[j].at[pl.ds(0, N - 1)]
        pltpu.make_async_copy(got, got, ur.at[j]).wait()

        def pick(k, carry):
            for e in range(4):
                at = lo + k * 4 + e
                t = recv_u[j][table[Q, at]].astype(F32)
                y_all[mine, h, at] = jnp.concatenate([t[:R], t[R:]], axis=1).astype(BF16)
            return carry

        lax.fori_loop(0, (hi - lo) // 4, pick, 0)
        part = y_all.at[mine, h, pl.ds(lo, hi - lo)]
        if s == 0:
            relays.append((j, h, send_y(part, j, 0, 1), send_y(part, j, 1, 3)))
        else:
            gathers.extend(send_y(part, j, way, k) for way, k in enumerate((2, 1, 3)))

    take(0)
    got = recv_b.at[pl.ds(0, X * C - 1)]
    pltpu.make_async_copy(got, got, br).wait()
    adam_sums = jnp.sum(recv_b[...], axis=0)
    scale = graft(0, adam_sums)
    send_back(0, 0, scale)
    send_back(0, 1, scale)
    take(1)
    scale = graft(1, adam_sums)
    send_back(1, 0, scale)
    send_back(1, 1, scale)
    for s in range(2):
        g = grad[s]
        left[s] = (
            lax.dot_general(g, g, (((1,), (1,)), ((), ())), preferred_element_type=F32) / T
        )
        right[s] = (
            lax.dot_general(g, g, (((0,), (0,)), ((), ())), preferred_element_type=F32) / T
        )
    gather(0, 0)
    forward()
    gather(0, 1)
    gather(1, 0)
    forward()
    gather(1, 1)

    for copy in gathers:
        copy.wait()
    for s in range(2):
        sent = send_g.at[s, pl.ds(0, N - 1)]
        pltpu.make_async_copy(sent, sent, gs.at[s]).wait()
    for j in range(OUT_CHUNKS):
        sent = send_u.at[j, pl.ds(0, N - 1)]
        pltpu.make_async_copy(sent, sent, us.at[j]).wait()
    sent = recv_a.at[pl.ds(0, Z - 1)]
    pltpu.make_async_copy(sent, sent, as_).wait()
    sent = recv_b.at[pl.ds(0, X * C - 1)]
    pltpu.make_async_copy(sent, sent, bs).wait()


def finish_kernel(
    y_all, moment, left, right, rank, update_out, moment_out, left_out, right_out, sem
):
    step = pl.program_id(0)
    copies = [
        pltpu.make_async_copy(left, left_out.at[0, 0], sem.at[0]),
        pltpu.make_async_copy(right, right_out.at[0, 0], sem.at[1]),
        pltpu.make_async_copy(moment, moment_out, sem.at[2]),
    ]

    @pl.when(step == 0)
    def _():
        for copy in copies:
            copy.start()

    for b in range(STEP_BANDS):
        for q in range(Q):
            for c in range(NC):
                at = rank[q, (step * STEP_BANDS + b) * NC + c]
                for h in range(2):
                    col = q * W + c * T + h * HW
                    update_out[b, :, col : col + HW] = y_all[q, h, at]

    @pl.when(step == BANDS // STEP_BANDS - 1)
    def _():
        for copy in copies:
            copy.wait()


def positions(where_v, q):
    owner, row, col = where_v[0], where_v[1], where_v[2]
    blocks = owner.shape[1]
    col = col // T
    piece = (row // T) * NC + col % NC
    here = (col // NC) == q
    code = lax.broadcasted_iota(jnp.int32, (1, blocks), 1) * N + piece
    owner = jnp.where(here, owner, N)
    match = owner == lax.broadcasted_iota(jnp.int32, (N, blocks), 0)
    first = jnp.min(jnp.where(match, code, 1 << 20), axis=1, keepdims=True)
    last = jnp.max(jnp.where(match, code, -1), axis=1, keepdims=True)
    has0 = last >= 0
    has1 = last > first
    p0 = jnp.where(has0, first % N, N)
    p1 = jnp.where(has1, last % N, N)
    sub = lax.broadcasted_iota(jnp.int32, (N, 128), 0)
    lane = lax.broadcasted_iota(jnp.int32, (N, 128), 1)

    def total(v):
        return jnp.sum(v, axis=0, keepdims=True)

    row0 = total(jnp.where(sub == lane, p0, 0))
    row1 = total(jnp.where(sub == lane, p1, 0))

    def before(row):
        return jnp.sum(jnp.where((lane < sub) & (row < N), 1, 0), axis=1, keepdims=True)

    rank0 = jnp.where(has0, before(row0), -1)
    rank1 = jnp.where(has1, SINGLE + before(row1), -1)
    owners = total(jnp.where((rank0 == lane) | (rank1 == lane), sub, 0))
    ranks = total(jnp.where(p0 == lane, rank0, 0) + jnp.where(p1 == lane, rank1, 0))
    return row0, row1, owners, ranks


def body(gradient, second_moment, left_root, right_root, block_owner, row_offset, col_offset):
    hbm = pl.BlockSpec(memory_space=pltpu.HBM)
    vmem = pl.BlockSpec(memory_space=pltpu.VMEM)
    smem = pl.BlockSpec(memory_space=pltpu.SMEM)
    dma = pltpu.SemaphoreType.DMA
    blocks = block_owner.shape[0]
    places = [v.reshape(1, blocks) for v in (block_owner, row_offset, col_offset)]
    operands = [
        pltpu.with_memory_space_constraint(v, pltpu.HBM)
        for v in (*places, gradient, second_moment, left_root[0, 0], right_root[0, 0])
    ]
    kept = pl.pallas_call(
        exchange_kernel,
        out_shape=[
            pltpu.VMEM((Q, 2, N, R, HW), BF16),
            pltpu.VMEM((BANDS, R, W), BF16),
            pltpu.VMEM((2, T, T), F32),
            pltpu.VMEM((2, T, T), F32),
            pltpu.SMEM((8, 128), jnp.int32),
        ],
        in_specs=[hbm] * 7,
        out_specs=[vmem] * 4 + [smem],
        scratch_shapes=[
            pltpu.VMEM((3, 1, blocks), jnp.int32),
            pltpu.VMEM((8, 128), jnp.int32),
            pltpu.SMEM((8, 128), jnp.int32),
            pltpu.VMEM((8, 128), jnp.int32),
            pltpu.VMEM((BANDS, R, W), BF16),
            pltpu.VMEM((BANDS, R, W), BF16),
            pltpu.VMEM((2, T, T), BF16),
            pltpu.VMEM((2, T, T), BF16),
            pltpu.VMEM((N + 1, 2 * R, HW), F32),
            pltpu.VMEM((N, R, 128), F32),
            pltpu.VMEM((2, N, 2 * R, HW), BF16),
            pltpu.VMEM((2, N, 2 * R, HW), BF16),
            pltpu.VMEM((2, T, T), BF16),
            pltpu.VMEM((2, T, T), F32),
            pltpu.VMEM((OUT_CHUNKS, N, 2 * R, 128), BF16),
            *[pltpu.VMEM((N, 2 * R, 128), BF16)] * OUT_CHUNKS,
            pltpu.VMEM((1, 128), F32),
            pltpu.VMEM((Z, 1, 128), F32),
            pltpu.VMEM((1, 128), F32),
            pltpu.VMEM((X * C, 1, 128), F32),
            dma((7,)),
            dma,
            dma((2,)),
            dma((2,)),
            dma,
            dma,
            dma,
            dma,
            dma((OUT_CHUNKS,)),
            dma((OUT_CHUNKS,)),
            dma((OUT_CHUNKS, Q)),
            dma((OUT_CHUNKS, Q)),
        ],
        compiler_params=pltpu.CompilerParams(
            collective_id=0, has_side_effects=True, vmem_limit_bytes=32 << 20
        ),
    )(*operands)

    return pl.pallas_call(
        finish_kernel,
        grid=(BANDS // STEP_BANDS,),
        out_shape=[
            jax.ShapeDtypeStruct((BANDS, R, Q * W), BF16),
            jax.ShapeDtypeStruct((BANDS, R, W), BF16),
            jax.ShapeDtypeStruct((1, 1, 2, T, T), F32),
            jax.ShapeDtypeStruct((1, 1, 2, T, T), F32),
        ],
        in_specs=[vmem] * 4 + [smem],
        out_specs=[pl.BlockSpec((STEP_BANDS, R, Q * W), lambda t: (t, 0, 0)), hbm, hbm, hbm],
        scratch_shapes=[dma((3,))],
        compiler_params=pltpu.CompilerParams(vmem_limit_bytes=16 << 20),
    )(*kept)


def solution(mesh):
    placed = P(None, "fsdp", "group")
    slots = P("fsdp", "group", None, None, None)
    return jax.shard_map(
        body,
        mesh=mesh,
        in_specs=(placed, placed, slots, slots, P(), P(), P()),
        out_specs=(P(None, "fsdp", None), placed, slots, slots),
        check_vma=False,
    )
```

```python
import functools

import jax
import jax.numpy as jnp
from jax import lax
from jax.experimental import pallas as pl
from jax.experimental.pallas import tpu as pltpu
from jax.sharding import PartitionSpec as P

MESH = pl.DeviceIdType.MESH
F32 = jnp.float32
BF16 = jnp.bfloat16

N = 64
X, Z, C = 4, 8, 2
Q = 4
T = 512
BANDS = 16
R = 8
W = 2048
NC = W // T
HW = T // 2
OUT_CHUNKS = 4
SINGLE = N - N // 4
STEP_BANDS = 8
EARLY = 7


def place(me):
    return lax.div(me, C * Z), lax.rem(lax.div(me, C), Z), lax.rem(me, C)


def near(me):
    x, _, c = place(me)
    return [
        lax.rem(x + dx, X) * (Z * C) + lax.rem(c + dc, C)
        for dx, dc in ((2, 0), (2, 1), (1, 0), (1, 1), (3, 0), (3, 1), (0, 1), (0, 0))
    ]


def others_far(me, fn, first, last):
    z = place(me)[1]
    same = near(me)

    def far(k, carry):
        half = (k + 1) // 2
        dz = jnp.where(k % 2 == 1, half, Z - half)
        row = lax.rem(z + 4 + dz, Z) * C
        for there in same:
            fn(there + row)
        return carry

    lax.fori_loop(first, last, far, 0)


def others_near(me, fn):
    z = place(me)[1]
    for there in near(me)[:-1]:
        fn(there + z * C)


def others(me, fn):
    others_far(me, fn, 0, Z - 1)
    others_near(me, fn)


def exchange_kernel(
    o_hbm, r0_hbm, c0_hbm, g_hbm, m_hbm, l_hbm, r_hbm, y_all, moment, left, right, table,
    where_v, idx_v, idx, table_v, gv, mv, lv, rv, pieces, apart, send_g, recv_g, grad, pre,
    send_u, ru0, ru1, ru2, ru3, sum_a, recv_a, sum_b, recv_b,
    load_sem, idx_sem, gs, gr, as_, ar, bs, br, us, ur, ys, yr,
):
    recv_u = (ru0, ru1, ru2, ru3)
    me = lax.axis_index("fsdp")
    mine = lax.axis_index("group")
    x, z, core = place(me)
    spot = x * C + core

    loads = [
        pltpu.make_async_copy(src, dst, load_sem.at[i])
        for i, (src, dst) in enumerate(
            [
                (g_hbm, gv), (m_hbm, mv), (l_hbm, lv), (r_hbm, rv),
                (o_hbm, where_v.at[0]), (r0_hbm, where_v.at[1]), (c0_hbm, where_v.at[2]),
            ]
        )
    ]
    for i in (4, 5, 6, 0, 1, 2, 3):
        loads[i].start()

    barrier = pltpu.get_barrier_semaphore()

    def greet(d):
        pl.semaphore_signal(barrier, inc=1, device_id={"fsdp": d}, device_id_type=MESH)

    others_far(me, greet, 0, 4)
    for k in range(1, Q):
        pl.semaphore_signal(
            barrier, inc=1, device_id={"group": lax.rem(mine + k, Q)}, device_id_type=MESH
        )

    for i in (4, 5, 6):
        loads[i].wait()
    row0, row1, _, _ = positions(where_v, mine)
    idx_v[0:1] = row0
    idx_v[1:2] = row1
    to_smem = pltpu.make_async_copy(idx_v, idx, idx_sem)
    to_smem.start()
    others_far(me, greet, 4, Z - 1)
    others_near(me, greet)

    loads[0].wait()

    def split(b, carry):
        rows = gv[b].astype(F32)
        for c in range(NC):
            for h in range(2):
                at = c * T + h * HW
                pieces[b * NC + c, h * R : (h + 1) * R] = rows[:, at : at + HW]
        return carry

    lax.fori_loop(0, BANDS, split, 0)
    pieces[N] = jnp.zeros((2 * R, HW), F32)
    to_smem.wait()

    def pack(s):
        def four(k, carry):
            for e in range(4):
                o = k * 4 + e
                send_g[s, o] = pieces[idx[s, o]].astype(BF16)
            return carry

        lax.fori_loop(0, N // 4, four, 0)

    pack(0)

    pl.semaphore_wait(barrier, N - 1 + Q - 1)

    def send_slot(s):
        def send(d):
            pltpu.make_async_remote_copy(
                send_g.at[s, d], recv_g.at[s, me], gs.at[s], gr.at[s],
                device_id={"fsdp": d}, device_id_type=MESH,
            ).start()

        return send

    others(me, send_slot(0))
    pack(1)

    loads[1].wait()

    def adam(b, carry):
        g = gv[b].astype(F32)
        m = mv[b].astype(F32)
        second = (0.95 * m + 0.05 * g * g).astype(BF16)
        moment[b] = second
        a = g / (jnp.sqrt(second.astype(F32)) + 1e-8)
        sq = a * a
        for c in range(NC):
            part = sq[:, c * T : c * T + 128]
            for i in range(1, T // 128):
                part = part + sq[:, c * T + i * 128 : c * T + (i + 1) * 128]
            apart[b * NC + c] = part
        return carry

    lax.fori_loop(0, BANDS, adam, 0)
    column = jnp.sum(jnp.sum(apart[...], axis=1), axis=1, keepdims=True)
    own_lane = lax.broadcasted_iota(jnp.int32, (N, 128), 0) == lax.broadcasted_iota(
        jnp.int32, (N, 128), 1
    )
    sum_a[...] = jnp.sum(jnp.where(own_lane, column, 0.0), axis=0, keepdims=True)
    recv_a[z] = sum_a[...]
    for dz in range(1, Z):
        pltpu.make_async_remote_copy(
            sum_a, recv_a.at[z], as_, ar,
            device_id={"fsdp": x * (Z * C) + lax.rem(z + dz, Z) * C + core}, device_id_type=MESH,
        ).start()
    others_far(me, send_slot(1), 0, 4)
    got = recv_a.at[pl.ds(0, Z - 1)]
    pltpu.make_async_copy(got, got, ar).wait()
    sum_b[...] = jnp.sum(recv_a[...], axis=0)
    recv_b[spot] = sum_b[...]

    def send_b(d):
        pltpu.make_async_remote_copy(
            sum_b, recv_b.at[spot], bs, br, device_id={"fsdp": d}, device_id_type=MESH
        ).start()

    others_near(me, send_b)
    others_far(me, send_slot(1), 4, Z - 1)
    others_near(me, send_slot(1))
    for q in range(Q):
        table_v[q : q + 1] = positions(where_v, q)[3]
    table_v[Q : Q + 1] = positions(where_v, mine)[2]
    to_table = pltpu.make_async_copy(table_v, table, idx_sem)
    to_table.start()
    to_table.wait()

    for s in range(2):
        recv_g[s, me] = send_g[s, me]

    loads[2].wait()
    loads[3].wait()

    group_rows = 8

    def take(s):
        got = recv_g.at[s, pl.ds(0, N - 1)]
        pltpu.make_async_copy(got, got, gr.at[s]).wait()

        def sort(t, carry):
            v = recv_g[s, pl.ds(t * group_rows, group_rows)].astype(F32)
            for h in range(2):
                rows = v[:, h * R : (h + 1) * R, :].reshape(group_rows * R, HW)
                grad[s, pl.ds(t * group_rows * R, group_rows * R), h * HW : (h + 1) * HW] = rows.astype(
                    BF16
                )
            return carry

        lax.fori_loop(0, N // group_rows, sort, 0)
        half = jnp.dot(lv[s], grad[s], preferred_element_type=F32).astype(BF16)
        pre[s] = jnp.dot(half, rv[s], preferred_element_type=F32)

    def graft(s, adam_sums):
        lane = lax.broadcasted_iota(jnp.int32, (1, 128), 1)
        a_sum = jnp.sum(jnp.where(lane == idx[s, me], adam_sums, 0.0), axis=1, keepdims=True)
        sq = jnp.sum(pre[s] * pre[s], axis=0, keepdims=True)
        p_mean = jnp.sum(sq, axis=1, keepdims=True) / (T * T)
        return jnp.sqrt(a_sum / (T * T) / (p_mean + 1e-6))

    def send_back(s, h, scale):
        j = s * 2 + h
        tiles = [
            (pre[s, :, pl.ds(h * HW + i * 128, 128)] * scale).reshape(N, R, 128) for i in range(2)
        ]
        send_u[j] = jnp.concatenate(tiles, axis=1).astype(BF16)

        def send(d):
            pltpu.make_async_remote_copy(
                send_u.at[j, d], recv_u[j].at[me], us.at[j], ur.at[j],
                device_id={"fsdp": d}, device_id_type=MESH,
            ).start()

        others(me, send)
        recv_u[j][me] = send_u[j, me]

    gathers = []
    relays = []

    def send_y(part, j, way, k):
        copy = pltpu.make_async_remote_copy(
            part, part, ys.at[j, way], yr.at[j, way],
            device_id={"group": lax.rem(mine + k, Q)}, device_id_type=MESH,
        )
        copy.start()
        return copy

    def forward():
        for j, h, right_copy, left_copy in relays:
            right_copy.wait_recv()
            gathers.append(send_y(y_all.at[lax.rem(mine + 3, Q), h, pl.ds(0, SINGLE // 2)], j, 2, 1))
            left_copy.wait_recv()
            gathers.append(
                send_y(y_all.at[lax.rem(mine + 1, Q), h, pl.ds(SINGLE // 2, SINGLE // 2)], j, 3, 3)
            )
            right_copy.wait_send()
            left_copy.wait_send()
        relays.clear()

    def gather(s, h):
        j = s * 2 + h
        lo, hi = (0, SINGLE) if s == 0 else (SINGLE, N)
        got = recv_u[j].at[pl.ds(0, N - 1)]
        pltpu.make_async_copy(got, got, ur.at[j]).wait()

        def pick(k, carry):
            for e in range(4):
                at = lo + k * 4 + e
                t = recv_u[j][table[Q, at]].astype(F32)
                y_all[mine, h, at] = jnp.concatenate([t[:R], t[R:]], axis=1).astype(BF16)
            return carry

        lax.fori_loop(0, (hi - lo) // 4, pick, 0)
        part = y_all.at[mine, h, pl.ds(lo, hi - lo)]
        if s == 0:
            relays.append((j, h, send_y(part, j, 0, 1), send_y(part, j, 1, 3)))
        else:
            gathers.extend(send_y(part, j, way, k) for way, k in enumerate((2, 1, 3)))

    take(0)
    got = recv_b.at[pl.ds(0, X * C - 1)]
    pltpu.make_async_copy(got, got, br).wait()
    adam_sums = jnp.sum(recv_b[...], axis=0)
    scale = graft(0, adam_sums)
    send_back(0, 0, scale)
    send_back(0, 1, scale)
    take(1)
    scale = graft(1, adam_sums)
    send_back(1, 0, scale)
    gather(0, 0)
    send_back(1, 1, scale)
    for s in range(2):
        g = grad[s]
        left[s] = (
            lax.dot_general(g, g, (((1,), (1,)), ((), ())), preferred_element_type=F32) / T
        )
        right[s] = (
            lax.dot_general(g, g, (((0,), (0,)), ((), ())), preferred_element_type=F32) / T
        )
    forward()
    gather(0, 1)
    gather(1, 0)
    forward()
    gather(1, 1)

    for copy in gathers:
        copy.wait()
    for s in range(2):
        sent = send_g.at[s, pl.ds(0, N - 1)]
        pltpu.make_async_copy(sent, sent, gs.at[s]).wait()
    for j in range(OUT_CHUNKS):
        sent = send_u.at[j, pl.ds(0, N - 1)]
        pltpu.make_async_copy(sent, sent, us.at[j]).wait()
    sent = recv_a.at[pl.ds(0, Z - 1)]
    pltpu.make_async_copy(sent, sent, as_).wait()
    sent = recv_b.at[pl.ds(0, X * C - 1)]
    pltpu.make_async_copy(sent, sent, bs).wait()


def finish_kernel(
    y_all, moment, left, right, rank, update_out, moment_out, left_out, right_out, sem
):
    step = pl.program_id(0)
    copies = [
        pltpu.make_async_copy(left, left_out.at[0, 0], sem.at[0]),
        pltpu.make_async_copy(right, right_out.at[0, 0], sem.at[1]),
        pltpu.make_async_copy(moment, moment_out, sem.at[2]),
    ]

    @pl.when(step == 0)
    def _():
        for copy in copies:
            copy.start()

    for b in range(STEP_BANDS):
        for q in range(Q):
            for c in range(NC):
                at = rank[q, (step * STEP_BANDS + b) * NC + c]
                for h in range(2):
                    col = q * W + c * T + h * HW
                    update_out[b, :, col : col + HW] = y_all[q, h, at]

    @pl.when(step == BANDS // STEP_BANDS - 1)
    def _():
        for copy in copies:
            copy.wait()


def positions(where_v, q):
    owner, row, col = where_v[0], where_v[1], where_v[2]
    blocks = owner.shape[1]
    col = col // T
    piece = (row // T) * NC + col % NC
    here = (col // NC) == q
    code = lax.broadcasted_iota(jnp.int32, (1, blocks), 1) * N + piece
    owner = jnp.where(here, owner, N)
    match = owner == lax.broadcasted_iota(jnp.int32, (N, blocks), 0)
    first = jnp.min(jnp.where(match, code, 1 << 20), axis=1, keepdims=True)
    last = jnp.max(jnp.where(match, code, -1), axis=1, keepdims=True)
    has0 = last >= 0
    has1 = last > first
    p0 = jnp.where(has0, first % N, N)
    p1 = jnp.where(has1, last % N, N)
    sub = lax.broadcasted_iota(jnp.int32, (N, 128), 0)
    lane = lax.broadcasted_iota(jnp.int32, (N, 128), 1)

    def total(v):
        return jnp.sum(v, axis=0, keepdims=True)

    row0 = total(jnp.where(sub == lane, p0, 0))
    row1 = total(jnp.where(sub == lane, p1, 0))

    def before(row):
        return jnp.sum(jnp.where((lane < sub) & (row < N), 1, 0), axis=1, keepdims=True)

    rank0 = jnp.where(has0, before(row0), -1)
    rank1 = jnp.where(has1, SINGLE + before(row1), -1)
    owners = total(jnp.where((rank0 == lane) | (rank1 == lane), sub, 0))
    ranks = total(jnp.where(p0 == lane, rank0, 0) + jnp.where(p1 == lane, rank1, 0))
    return row0, row1, owners, ranks


def body(gradient, second_moment, left_root, right_root, block_owner, row_offset, col_offset):
    hbm = pl.BlockSpec(memory_space=pltpu.HBM)
    vmem = pl.BlockSpec(memory_space=pltpu.VMEM)
    smem = pl.BlockSpec(memory_space=pltpu.SMEM)
    dma = pltpu.SemaphoreType.DMA
    blocks = block_owner.shape[0]
    places = [v.reshape(1, blocks) for v in (block_owner, row_offset, col_offset)]
    operands = [
        pltpu.with_memory_space_constraint(v, pltpu.HBM)
        for v in (*places, gradient, second_moment, left_root[0, 0], right_root[0, 0])
    ]
    kept = pl.pallas_call(
        exchange_kernel,
        out_shape=[
            pltpu.VMEM((Q, 2, N, R, HW), BF16),
            pltpu.VMEM((BANDS, R, W), BF16),
            pltpu.VMEM((2, T, T), F32),
            pltpu.VMEM((2, T, T), F32),
            pltpu.SMEM((8, 128), jnp.int32),
        ],
        in_specs=[hbm] * 7,
        out_specs=[vmem] * 4 + [smem],
        scratch_shapes=[
            pltpu.VMEM((3, 1, blocks), jnp.int32),
            pltpu.VMEM((8, 128), jnp.int32),
            pltpu.SMEM((8, 128), jnp.int32),
            pltpu.VMEM((8, 128), jnp.int32),
            pltpu.VMEM((BANDS, R, W), BF16),
            pltpu.VMEM((BANDS, R, W), BF16),
            pltpu.VMEM((2, T, T), BF16),
            pltpu.VMEM((2, T, T), BF16),
            pltpu.VMEM((N + 1, 2 * R, HW), F32),
            pltpu.VMEM((N, R, 128), F32),
            pltpu.VMEM((2, N, 2 * R, HW), BF16),
            pltpu.VMEM((2, N, 2 * R, HW), BF16),
            pltpu.VMEM((2, T, T), BF16),
            pltpu.VMEM((2, T, T), F32),
            pltpu.VMEM((OUT_CHUNKS, N, 2 * R, 128), BF16),
            *[pltpu.VMEM((N, 2 * R, 128), BF16)] * OUT_CHUNKS,
            pltpu.VMEM((1, 128), F32),
            pltpu.VMEM((Z, 1, 128), F32),
            pltpu.VMEM((1, 128), F32),
            pltpu.VMEM((X * C, 1, 128), F32),
            dma((7,)),
            dma,
            dma((2,)),
            dma((2,)),
            dma,
            dma,
            dma,
            dma,
            dma((OUT_CHUNKS,)),
            dma((OUT_CHUNKS,)),
            dma((OUT_CHUNKS, Q)),
            dma((OUT_CHUNKS, Q)),
        ],
        compiler_params=pltpu.CompilerParams(
            collective_id=0, has_side_effects=True, vmem_limit_bytes=32 << 20
        ),
    )(*operands)

    return pl.pallas_call(
        finish_kernel,
        grid=(BANDS // STEP_BANDS,),
        out_shape=[
            jax.ShapeDtypeStruct((BANDS, R, Q * W), BF16),
            jax.ShapeDtypeStruct((BANDS, R, W), BF16),
            jax.ShapeDtypeStruct((1, 1, 2, T, T), F32),
            jax.ShapeDtypeStruct((1, 1, 2, T, T), F32),
        ],
        in_specs=[vmem] * 4 + [smem],
        out_specs=[pl.BlockSpec((STEP_BANDS, R, Q * W), lambda t: (t, 0, 0)), hbm, hbm, hbm],
        scratch_shapes=[dma((3,))],
        compiler_params=pltpu.CompilerParams(vmem_limit_bytes=16 << 20),
    )(*kept)


def solution(mesh):
    placed = P(None, "fsdp", "group")
    slots = P("fsdp", "group", None, None, None)
    return jax.shard_map(
        body,
        mesh=mesh,
        in_specs=(placed, placed, slots, slots, P(), P(), P()),
        out_specs=(P(None, "fsdp", None), placed, slots, slots),
        check_vma=False,
    )
```
